32 devices in a mesh: dp: 4 (over y, x), ctx: 4 (over z), tensor: 2 (over core).
Axes of the slice: x: 2, y: 2, z: 4, core: 2. Of those that a mesh axis runs over, the one named last changes fastest.
Arguments:
- layer_input: bfloat16 [4096, 2048], P(('dp', 'ctx', 'tensor')), may hold values from -6 to 6
- segments: int32 [4096], P(('dp', 'ctx')), may hold values from 0 to 3, as said below
- attn_gain: bfloat16 [2048], P(('dp', 'ctx')), may hold values from 0.5 to 1.5
- query_weight: bfloat16 [2048, 2048], P(('dp', 'ctx'), 'tensor'), may hold values from -0.015625 to 0.015625
- key_weight: bfloat16 [2048, 2048], P(('dp', 'ctx'), 'tensor'), may hold values from -0.125 to 0.125
- value_weight: bfloat16 [2048, 2048], P(('dp', 'ctx'), 'tensor'), may hold values from -0.125 to 0.125
- output_weight: bfloat16 [2048, 2048], P('tensor', ('dp', 'ctx')), may hold values from -2 to 2
- bias_table: float32 [32, 32], P(None, 'tensor'), may hold values from -4 to 4
- ff_gain: bfloat16 [2048], P(('dp', 'ctx')), may hold values from 0.5 to 1.5
- gate_weight: bfloat16 [2048, 5120], P(('dp', 'ctx'), 'tensor'), may hold values from -0.125 to 0.125
- up_weight: bfloat16 [2048, 5120], P(('dp', 'ctx'), 'tensor'), may hold values from -0.125 to 0.125
- down_weight: bfloat16 [5120, 2048], P('tensor', ('dp', 'ctx')), may hold values from -0.078125 to 0.078125
- cotangent: bfloat16 [4096, 2048], P(('dp', 'ctx', 'tensor')), may hold values from -6 to 6
Outputs:
- block_output: bfloat16 [4096, 2048], P(('dp', 'ctx', 'tensor'))
- input_grads: bfloat16 [4096, 2048], P(('dp', 'ctx', 'tensor'))
- attn_gain_grads: float32 [2048], replicated
- query_grads: float32 [2048, 2048], P(('dp', 'ctx'), 'tensor')
- key_grads: float32 [2048, 2048], P(('dp', 'ctx'), 'tensor')
- value_grads: float32 [2048, 2048], P(('dp', 'ctx'), 'tensor')
- output_grads: float32 [2048, 2048], P('tensor', ('dp', 'ctx'))
- bias_grads: float32 [32, 32], replicated
- ff_gain_grads: float32 [2048], replicated
- gate_grads: float32 [2048, 5120], P(('dp', 'ctx'), 'tensor')
- up_grads: float32 [2048, 5120], P(('dp', 'ctx'), 'tensor')
- down_grads: float32 [5120, 2048], P('tensor', ('dp', 'ctx'))
- rms_stats: float32 [2], replicated
The draws below stay inside these ranges and needn't reach their ends.
Inputs may be any that keep to these rules, and one draw needn't show every extreme that they name: `segments`: each sequence of 1024 tokens holds document 1, then document 2, then document 3, then padding 0; document 1 lies within the first 256 tokens, document 2 ends within the last 256 tokens, and every sequence ends with at least one padding token.
All inputs are finite; a program needn't handle non-finite values.
Results may differ from the reference program's by a relative error of at most 0.018.
Values may be sent and summed in bfloat16 or wider, within the bound.
No kernel may reach another device: no remote copies, remote signals or barrier semaphores. Data moves between devices by JAX's collectives and lax.ppermute only.
A program may use at most 256 MiB of HBM per device.

```python
import jax
import jax.numpy as jnp
from jax import lax

D = 2048
H = 32
DH = 64
FF = 5120
NB = 32
GROUP = 256
LEN = 1024
TOKENS = 4096


def draw_segments(key, part):
    key = jax.random.fold_in(key, 11)
    count = TOKENS // LEN
    seq_keys = jax.random.split(key, count)

    def one_sequence(seq_key):
        first_key, second_key, third_key = jax.random.split(seq_key, 3)
        start_long = jax.random.randint(first_key, (), 1, GROUP)
        end_long = jax.random.randint(second_key, (), LEN - GROUP + 1, LEN - 1)
        end_last = jax.random.randint(third_key, (), end_long + 1, LEN)
        places = jnp.arange(LEN, dtype=jnp.int32)
        ident = jnp.where(places < start_long, 1, jnp.where(places < end_long, 2, jnp.where(places < end_last, 3, 0)))
        return ident.astype(jnp.int32)
    return jax.vmap(one_sequence)(seq_keys).reshape(-1)


def levels(rng, shape, shards, low, high):
    loudness, own = 1.0, jax.random.fold_in(rng, 6)
    for axis_at, parts in shards:
        draws = jnp.exp(jax.random.uniform(jax.random.fold_in(own, axis_at), (parts,), jnp.float32, low / len(shards), high / len(shards)))
        loudness = loudness * jnp.repeat(draws, shape[axis_at] // parts).reshape([-1 if axis == axis_at else 1 for axis in range(len(shape))])
    return loudness


def centred(key, extent, spread, reach, cuts=(), kind=jnp.bfloat16):
    factor_of = levels(key, extent, cuts, -0.22, 0.18) if cuts else 1.0
    result = jax.random.normal(key, extent, jnp.float32) * spread * factor_of
    return jnp.minimum(jnp.maximum(result, -reach), reach).astype(kind)


def setup_inputs(seed: int = 0) -> dict:
    seeds = jax.random.split(jax.random.key(seed), 14)
    layer_input = centred(seeds[0], (TOKENS, D), 1.0, 6.0, ((0, 32),))
    segments = draw_segments(jax.random.fold_in(seeds[13], 71), 0)
    attn_gain = jnp.clip(1.0 + 0.1 * jax.random.normal(seeds[2], (D,), jnp.float32), 0.5, 1.5).astype(jnp.bfloat16)
    query_weight = centred(seeds[3], (D, H * DH), (D * DH) ** -0.5, 0.015625, ((0, 16), (1, 2)))
    key_weight = centred(seeds[4], (D, H * DH), D ** -0.5, 0.125, ((0, 16), (1, 2)))
    value_weight = centred(seeds[5], (D, H * DH), D ** -0.5, 0.125, ((0, 16), (1, 2)))
    output_weight = centred(seeds[6], (H * DH, D), (max(H * DH // 256, 1)) ** -0.5, 2.0, ((0, 2), (1, 16)))
    bias_table = centred(seeds[7], (NB, H), 1.0, 4.0, ((1, 2),), jnp.float32)
    ff_gain = jnp.clip(1.0 + 0.1 * jax.random.normal(seeds[8], (D,), jnp.float32), 0.5, 1.5).astype(jnp.bfloat16)
    gate_weight = centred(seeds[9], (D, FF), D ** -0.5, 0.125, ((0, 16), (1, 2)))
    up_weight = centred(seeds[10], (D, FF), D ** -0.5, 0.125, ((0, 16), (1, 2)))
    down_weight = centred(seeds[11], (FF, D), FF ** -0.5, 0.078125, ((0, 2), (1, 16)))
    cotangent = centred(seeds[12], (TOKENS, D), 1.0, 6.0, ((0, 32),))
    return dict(layer_input=layer_input, segments=segments, attn_gain=attn_gain, query_weight=query_weight, key_weight=key_weight, value_weight=value_weight, output_weight=output_weight, bias_table=bias_table, ff_gain=ff_gain, gate_weight=gate_weight, up_weight=up_weight, down_weight=down_weight, cotangent=cotangent)


edge_list = (12, 16, 23, 32, 46, 64, 91)
exact_span = 8
eps = 1e-06
highest = lax.Precision.HIGHEST

@jax.custom_vjp
def low(v):
    return lax.optimization_barrier(v.astype(jnp.bfloat16)).astype(jnp.float32)

@jax.custom_vjp
def low_back(v):
    return v

def low_keep(v):
    return (low(v), None)

def low_pass(kept, grad):
    return (grad,)

def back_keep(v):
    return (v, None)

def back_low(kept, grad):
    return (low(grad),)
low.defvjp(low_keep, low_pass)
low_back.defvjp(back_keep, back_low)

def bucket_of(relative):
    distance = jnp.abs(relative)
    coarse = jnp.full_like(distance, exact_span)
    for edge in edge_list:
        coarse = coarse + (distance >= edge).astype(jnp.int32)
    nearby = jnp.where(distance < exact_span, distance, coarse)
    return (nearby + jnp.where(relative > 0, NB // 2, 0)).astype(jnp.int32)

def rms_norm(values, gain):
    scale = lax.rsqrt(lax.optimization_barrier(jnp.mean(values * values, axis=-1, keepdims=True)) + eps)
    return values * scale * gain

def sequence_forward(params, seq_input, seq_segments, buckets):
    attn_gain, query_weight, key_weight, value_weight, output_weight, bias_table, ff_gain, gate_weight, up_weight, down_weight = params
    first_normalized_input = low(rms_norm(seq_input, attn_gain))
    query = low(low_back(jnp.dot(first_normalized_input, query_weight, precision=highest)))
    key = low(low_back(jnp.dot(first_normalized_input, key_weight, precision=highest)))
    value = low(low_back(jnp.dot(first_normalized_input, value_weight, precision=highest)))
    allowed = seq_segments[:, None] == seq_segments[None, :]

    def one_head(head):
        start = (head * DH).astype(jnp.int32)
        query_h = lax.dynamic_slice_in_dim(query, start, DH, 1)
        key_h = lax.dynamic_slice_in_dim(key, start, DH, 1)
        value_h = lax.dynamic_slice_in_dim(value, start, DH, 1)
        column = lax.dynamic_index_in_dim(bias_table, head, 1, keepdims=False)
        scores = jnp.dot(query_h, key_h.T, precision=highest) + column[buckets]
        scores = low_back(scores)
        scores = jnp.where(allowed, scores, -1e+30)
        top = lax.optimization_barrier(jnp.max(scores, axis=1, keepdims=True))
        expo = jnp.exp(scores - top)
        probs = expo / lax.optimization_barrier(jnp.sum(expo, axis=1, keepdims=True))
        return jnp.dot(low(probs), value_h, precision=highest)
    stacked = lax.map(jax.checkpoint(one_head), jnp.arange(H, dtype=jnp.int32))
    mixed = jnp.transpose(stacked, (1, 0, 2)).reshape(LEN, H * DH)
    mixed = low(low_back(mixed))
    first_hidden_state = seq_input + low_back(jnp.dot(mixed, output_weight, precision=highest))
    second_normalized_input = low(rms_norm(first_hidden_state, ff_gain))
    gate = low_back(jnp.dot(second_normalized_input, gate_weight, precision=highest))
    upper = low_back(jnp.dot(second_normalized_input, up_weight, precision=highest))
    inner = low(jax.nn.gelu(gate, approximate=True) * upper)
    return first_hidden_state + low_back(jnp.dot(inner, down_weight, precision=highest))

def reference(layer_input, segments, attn_gain, query_weight, key_weight, value_weight, output_weight, bias_table, ff_gain, gate_weight, up_weight, down_weight, cotangent):
    count = TOKENS // LEN
    params = tuple((item.astype(jnp.float32) for item in (attn_gain, query_weight, key_weight, value_weight, output_weight, bias_table, ff_gain, gate_weight, up_weight, down_weight)))
    positions = jnp.arange(LEN, dtype=jnp.int32)
    buckets = bucket_of(positions[None, :] - positions[:, None])
    inputs_seq = layer_input.astype(jnp.float32).reshape(count, LEN, D)
    cotangent_seq = cotangent.astype(jnp.float32).reshape(count, LEN, D)
    segments_seq = segments.reshape(count, LEN)

    def step(totals, items):
        seq_input, seq_segments, seq_cot = items
        output, pullback = jax.vjp(lambda inp, prm: sequence_forward(prm, inp, seq_segments, buckets), seq_input, params)
        input_grad, param_grads = pullback(seq_cot)
        totals = jax.tree.map(jnp.add, totals, param_grads)
        return (totals, (output, input_grad))
    zeros = jax.tree.map(jnp.zeros_like, params)
    totals, (outputs, input_grads) = lax.scan(step, zeros, (inputs_seq, segments_seq, cotangent_seq))
    block_output = outputs.reshape(TOKENS, D).astype(jnp.bfloat16)
    input_low = input_grads.reshape(TOKENS, D).astype(jnp.bfloat16)
    valid = (segments != 0).astype(jnp.float32)
    number = jnp.sum(valid) * D
    out_values = block_output.astype(jnp.float32)
    grad_values = input_low.astype(jnp.float32)
    first = jnp.sqrt(jnp.sum(valid * lax.optimization_barrier(jnp.sum(out_values * out_values, axis=1))) / number)
    second = jnp.sqrt(jnp.sum(valid * lax.optimization_barrier(jnp.sum(grad_values * grad_values, axis=1))) / number)
    rms_stats = jnp.stack([first, second])
    gain_one, query_g, key_g, value_g, output_g, bias_g, gain_two, gate_g, up_g, down_g = totals
    return (block_output, input_low, gain_one, query_g, key_g, value_g, output_g, bias_g, gain_two, gate_g, up_g, down_g, rms_stats)
```

```python
import functools

import jax
import jax.numpy as jnp
from jax import lax
from jax.experimental import pallas as pl
from jax.experimental.pallas import tpu as pltpu
from jax.sharding import PartitionSpec as P

NB = 32
DH = 64
edge_list = (12, 16, 23, 32, 46, 64, 91)
exact_span = 8
eps = 1e-06
highest = lax.Precision.HIGHEST
bf16 = jnp.bfloat16
f32 = jnp.float32

TQ = 256
REACH = 128
SPAN = TQ + 2 * REACH
WIDE = 1024


def bucket_of(relative):
    distance = jnp.abs(relative)
    coarse = jnp.full_like(distance, exact_span)
    for edge in edge_list:
        coarse = coarse + (distance >= edge).astype(jnp.int32)
    nearby = jnp.where(distance < exact_span, distance, coarse)
    return nearby + jnp.where(relative > 0, NB // 2, 0)


def lane_buckets():
    lane = jnp.arange(WIDE, dtype=jnp.int32)
    ahead = jnp.where(lane < TQ, lane, lane - WIDE)
    onehot = bucket_of(-ahead - REACH)[:, None] == jnp.arange(NB, dtype=jnp.int32)[None, :]
    return onehot.astype(f32)


def dot_nt(a, b):
    return lax.dot_general(a, b, (((1,), (1,)), ((), ())), preferred_element_type=f32)


def dot_nn(a, b):
    return lax.dot_general(a, b, (((1,), (0,)), ((), ())), preferred_element_type=f32)


def tile_range(tile, seq_len):
    start = tile * TQ
    low, high = max(0, start - REACH), min(seq_len, start + TQ + REACH)
    return start, low, high, low - (start - REACH), high - (start - REACH)


def tile_scores(key, query, strip_ref, far, seg_col, seg_row, tile, seq_len):
    start, low, high, strip_low, strip_high = tile_range(tile, seq_len)
    scores = dot_nt(key, query)
    parts = []
    if low > 0:
        parts.append(scores[:low] + far[0])
    parts.append(scores[low:high] + strip_ref[strip_low:strip_high])
    if high < seq_len:
        parts.append(scores[high:] + far[1])
    scores = jnp.concatenate(parts, axis=0) if len(parts) > 1 else parts[0]
    return jnp.where(seg_col == seg_row[:, start : start + TQ], scores, -1e30)


def make_strip(strip_ref, vector):
    tall = jnp.broadcast_to(vector, (SPAN, WIDE))
    strip_ref[...] = pltpu.roll(tall, 0, 1, stride=1, stride_axis=0)[:, :TQ]


def fold_diagonals(acc_ref):
    rest = jnp.zeros((8, WIDE - TQ), f32)
    groups = jnp.zeros((8, WIDE), f32)
    for at in range(0, SPAN, 8):
        wide = jnp.concatenate([acc_ref[at : at + 8, :], rest], axis=1)
        groups = groups + pltpu.roll(wide, (WIDE - at) % WIDE, 1)
    diagonals = groups[0:1]
    for row in range(1, 8):
        diagonals = diagonals + pltpu.roll(groups[row : row + 1], WIDE - row, 1)
    return diagonals


def attend_kernel(
    seq_len, q_ref, k_ref, v_ref, segc_ref, segr_ref, vec_ref, far_ref, mix_ref, lse_ref, strip_ref
):
    seg_col = segc_ref[...]
    seg_row = segr_ref[...]
    pair = pl.program_id(0)
    value_t = v_ref[...].T
    for half in range(2):
        make_strip(strip_ref, vec_ref[0, half : half + 1, :])
        far = (far_ref[2 * pair + half, 0], far_ref[2 * pair + half, 1])
        lanes = slice(half * DH, (half + 1) * DH)
        key = k_ref[:, lanes]
        for tile in range(seq_len // TQ):
            rows = slice(tile * TQ, (tile + 1) * TQ)
            query = q_ref[rows, lanes]
            scores = tile_scores(key, query, strip_ref, far, seg_col, seg_row, tile, seq_len)
            top = jnp.max(scores, axis=0, keepdims=True)
            expo = jnp.exp(scores - top)
            total = jnp.sum(expo, axis=0, keepdims=True)
            mixed_t = dot_nn(value_t[lanes, :], expo.astype(bf16)) * (1.0 / total)
            mix_ref[rows, lanes] = mixed_t.T.astype(bf16)
            lse_ref[0, half : half + 1, rows] = top + jnp.log(total)


def attend_back_kernel(
    seq_len,
    q_ref,
    k_ref,
    v_ref,
    do_ref,
    segc_ref,
    segr_ref,
    vec_ref,
    far_ref,
    lse_ref,
    dq_ref,
    dk_ref,
    dv_ref,
    diag_ref,
    farsum_ref,
    strip_ref,
    acc_ref,
    dk_acc,
    dv_acc,
):
    seg_col = segc_ref[...]
    seg_row = segr_ref[...]
    pair = pl.program_id(0)
    key_t = k_ref[...].T
    for half in range(2):
        make_strip(strip_ref, vec_ref[0, half : half + 1, :])
        far = (far_ref[2 * pair + half, 0], far_ref[2 * pair + half, 1])
        lanes = slice(half * DH, (half + 1) * DH)
        key = k_ref[:, lanes]
        value = v_ref[:, lanes]
        acc_ref[...] = jnp.zeros_like(acc_ref)
        far_before = jnp.zeros((1, TQ), f32)
        far_after = jnp.zeros((1, TQ), f32)
        for tile in range(seq_len // TQ):
            start, low, high, strip_low, strip_high = tile_range(tile, seq_len)
            rows = slice(start, start + TQ)
            query = q_ref[rows, lanes]
            mixed_grad = do_ref[rows, lanes]
            scores = tile_scores(key, query, strip_ref, far, seg_col, seg_row, tile, seq_len)
            probs = jnp.exp(scores - lse_ref[0, half : half + 1, rows])
            prob_grad = dot_nt(value, mixed_grad)
            centre = jnp.sum(probs * prob_grad, axis=0, keepdims=True)
            score_grad = probs * (prob_grad - centre)
            rounded = score_grad.astype(bf16)
            value_g = dot_nn(probs.astype(bf16), mixed_grad)
            key_g = dot_nn(rounded, query)
            if tile == 0:
                dv_acc[...] = value_g
                dk_acc[...] = key_g
            else:
                dv_acc[...] += value_g
                dk_acc[...] += key_g
            dq_ref[rows, lanes] = dot_nn(key_t[lanes, :], rounded).T.astype(bf16)
            acc_ref[strip_low:strip_high, :] += score_grad[low:high]
            if low > 0:
                far_before = far_before + jnp.sum(score_grad[:low], axis=0, keepdims=True)
            if high < seq_len:
                far_after = far_after + jnp.sum(score_grad[high:], axis=0, keepdims=True)
        dk_ref[:, lanes] = dk_acc[...].astype(bf16)
        dv_ref[:, lanes] = dv_acc[...].astype(bf16)
        diag_ref[0, half : half + 1, :] = fold_diagonals(acc_ref)
        farsum_ref[0, half : half + 1, 0:TQ] = far_before
        farsum_ref[0, half : half + 1, TQ : 2 * TQ] = far_after


def kernel_params():
    return pltpu.CompilerParams(vmem_limit_bytes=56 * 1024 * 1024)


def attention_specs(seq_len, pairs):
    wide = lambda at: pl.BlockSpec((seq_len, 2 * DH), lambda p, at=at: (0, at * pairs + p))
    seg_c = pl.BlockSpec((seq_len, 1), lambda p: (0, 0))
    seg_r = pl.BlockSpec((1, seq_len), lambda p: (0, 0))
    vec = pl.BlockSpec((1, 2, WIDE), lambda p: (p, 0, 0))
    far = pl.BlockSpec(memory_space=pltpu.SMEM)
    lse = pl.BlockSpec((1, 2, seq_len), lambda p: (p, 0, 0))
    return wide, seg_c, seg_r, vec, far, lse


def attend(qkv, segs, vectors, far):
    seq_len = qkv.shape[0]
    pairs = vectors.shape[0]
    wide, seg_c, seg_r, vec, far_spec, lse = attention_specs(seq_len, pairs)
    work = pairs * 2 * seq_len * seq_len
    return pl.pallas_call(
        functools.partial(attend_kernel, seq_len),
        grid=(pairs,),
        in_specs=[wide(0), wide(1), wide(2), seg_c, seg_r, vec, far_spec],
        out_specs=[wide(0), lse],
        out_shape=[
            jax.ShapeDtypeStruct((seq_len, pairs * 2 * DH), bf16),
            jax.ShapeDtypeStruct((pairs, 2, seq_len), f32),
        ],
        scratch_shapes=[pltpu.VMEM((SPAN, TQ), f32)],
        compiler_params=kernel_params(),
        cost_estimate=pl.CostEstimate(
            flops=16 * DH * work, bytes_accessed=8 * seq_len * pairs * DH, transcendentals=work
        ),
        name="attend",
    )(qkv, qkv, qkv, segs[:, None], segs[None, :], vectors, far)


def attend_back(qkv, mixed_grad, segs, vectors, far, lse_rows):
    seq_len = qkv.shape[0]
    pairs = vectors.shape[0]
    wide, seg_c, seg_r, vec, far_spec, lse = attention_specs(seq_len, pairs)
    work = pairs * 2 * seq_len * seq_len
    heads_shape = jax.ShapeDtypeStruct((seq_len, pairs * 2 * DH), bf16)
    return pl.pallas_call(
        functools.partial(attend_back_kernel, seq_len),
        grid=(pairs,),
        in_specs=[wide(0), wide(1), wide(2), wide(0), seg_c, seg_r, vec, far_spec, lse],
        out_specs=[
            wide(0),
            wide(0),
            wide(0),
            vec,
            pl.BlockSpec((1, 2, 2 * TQ), lambda p: (p, 0, 0)),
        ],
        out_shape=[
            heads_shape,
            heads_shape,
            heads_shape,
            jax.ShapeDtypeStruct((pairs, 2, WIDE), f32),
            jax.ShapeDtypeStruct((pairs, 2, 2 * TQ), f32),
        ],
        scratch_shapes=[
            pltpu.VMEM((SPAN, TQ), f32),
            pltpu.VMEM((SPAN, TQ), f32),
            pltpu.VMEM((seq_len, DH), f32),
            pltpu.VMEM((seq_len, DH), f32),
        ],
        compiler_params=kernel_params(),
        cost_estimate=pl.CostEstimate(
            flops=40 * DH * work, bytes_accessed=16 * seq_len * pairs * DH, transcendentals=work
        ),
        name="attend_back",
    )(qkv, qkv, qkv, mixed_grad, segs[:, None], segs[None, :], vectors, far, lse_rows)


def shift(value, axis, by):
    size = lax.axis_size(axis)
    return lax.ppermute(value, axis, [(i, (i + by) % size) for i in range(size)])


def block_at(stack, at):
    return lax.dynamic_index_in_dim(stack, at, 0, keepdims=False)


def place(stack, block, at):
    return lax.dynamic_update_slice(stack, block[None], (at,) + (jnp.int32(0),) * block.ndim)


def gather_axis(block, axis):
    size, me = lax.axis_size(axis), lax.axis_index(axis)
    stack = place(jnp.zeros((size,) + block.shape, block.dtype), block, me)
    for k in range(1, size):
        stack = place(stack, shift(block, axis, k), (me - k) % size)
    return stack


def exchange_axis(block_of, axis):
    size, me = lax.axis_size(axis), lax.axis_index(axis)
    own = block_of(me)
    stack = place(jnp.zeros((size,) + own.shape, own.dtype), own, me)
    for k in range(1, size):
        stack = place(stack, shift(block_of((me + k) % size), axis, k), (me - k) % size)
    return stack


def scatter_sum_axis(block_of, axis):
    size, me = lax.axis_size(axis), lax.axis_index(axis)
    arrived = [shift(block_of((me + k) % size).astype(bf16), axis, k) for k in range(1, size)]
    total = block_of(me).astype(f32)
    for block in arrived:
        total = total + block.astype(f32)
    return total


def gather_tokens(rows):
    parts, pieces = lax.axis_size("tensor"), lax.axis_size("ctx")
    t, z = lax.axis_index("tensor"), lax.axis_index("ctx")
    stack = jnp.zeros((pieces * parts,) + rows.shape, rows.dtype)
    for k in range(pieces):
        block = shift(rows, "ctx", k) if k else rows
        at = (z - k) % pieces
        stack = place(stack, block, at * parts + t)
        for j in range(1, parts):
            stack = place(stack, shift(block, "tensor", j), at * parts + (t - j) % parts)
    return stack.reshape(-1, rows.shape[1])


def scatter_tokens(partial):
    parts, pieces = lax.axis_size("tensor"), lax.axis_size("ctx")
    stack = partial.reshape(pieces, parts, -1, partial.shape[1])
    pieces_sum = scatter_sum_axis(
        lambda j: lax.dynamic_index_in_dim(stack, j, 1, keepdims=False), "tensor"
    )
    return scatter_sum_axis(lambda j: block_at(pieces_sum, j), "ctx")


def gather_weight(weights):
    pieces = lax.axis_size("ctx")

    def block_of(j):
        columns = [
            lax.dynamic_slice_in_dim(w, j * (w.shape[1] // pieces), w.shape[1] // pieces, 1)
            for w in weights
        ]
        return jnp.concatenate(columns, axis=1) if len(columns) > 1 else columns[0]

    stack = exchange_axis(block_of, "ctx")
    stack = stack.reshape(-1, stack.shape[-1])
    return gather_axis(stack, "dp").reshape(-1, stack.shape[-1])


def scatter_weight(grad, widths):
    dps, pieces = lax.axis_size("dp"), lax.axis_size("ctx")
    stack = grad.reshape(dps, -1, grad.shape[1])
    mine = scatter_sum_axis(lambda j: block_at(stack, j), "dp")
    mine = mine.reshape(pieces, -1, grad.shape[1])
    back = exchange_axis(lambda j: block_at(mine, j).astype(bf16), "ctx")
    outs, at = [], 0
    for width in widths:
        part = back[:, :, at : at + width].astype(f32)
        outs.append(jnp.transpose(part, (1, 0, 2)).reshape(part.shape[1], -1))
        at += width
    return outs


def root_mean_square_backward(grad, normalized, scale, gain):
    scaled = grad * gain
    return scale * (scaled - normalized * jnp.mean(scaled * normalized, axis=-1, keepdims=True))


def mm(a, b):
    return jnp.dot(a, b, preferred_element_type=f32)


def mm_nt(a, b):
    return dot_nt(a, b)


def mm_tn(a, b):
    return lax.dot_general(a, b, (((0,), (0,)), ((), ())), preferred_element_type=f32)


def inverse_scale(values):
    return lax.rsqrt(jnp.mean(values * values, axis=1, keepdims=True) + eps)


def shards(
    layer_input,
    segments,
    attn_gain,
    query_weight,
    key_weight,
    value_weight,
    output_weight,
    bias_table,
    ff_gain,
    gate_weight,
    up_weight,
    down_weight,
    cotangent,
):
    parts, pieces, dps = lax.axis_size("tensor"), lax.axis_size("ctx"), lax.axis_size("dp")
    t, z, s = lax.axis_index("tensor"), lax.axis_index("ctx"), lax.axis_index("dp")
    rows, width = layer_input.shape
    seq_len = rows * parts * pieces
    part_heads = bias_table.shape[1]
    heads = part_heads // pieces
    head_cols = heads * DH

    x_seq = gather_tokens(layer_input)
    gains = gather_axis(gather_axis(jnp.stack([attn_gain, ff_gain]), "ctx"), "dp")
    gains = jnp.transpose(gains, (2, 0, 1, 3)).reshape(2, width).astype(f32)
    gain_one, gain_two = gains[0:1], gains[1:2]
    w_qkv = gather_weight([query_weight, key_weight, value_weight])
    output_t = gather_axis(output_weight.T, "ctx")
    w_out = gather_axis(output_t, "dp").reshape(width, -1)
    w_gu = gather_weight([gate_weight, up_weight])
    w_down = gather_weight([down_weight.T])
    dy_seq = gather_tokens(cotangent)
    segs = gather_axis(segments, "ctx").reshape(seq_len)

    own_table = lax.dynamic_slice_in_dim(bias_table, z * heads, heads, 1)
    lanes_onehot = lane_buckets()
    vectors = jnp.dot(lanes_onehot, own_table, precision=highest).T.reshape(heads // 2, 2, WIDE)
    far = jnp.stack([own_table[NB // 2 - 1], own_table[NB - 1]], axis=1)

    x_wide = x_seq.astype(f32)
    normed_seq = (x_wide * inverse_scale(x_wide) * gain_one).astype(bf16)
    qkv = mm(normed_seq, w_qkv).astype(bf16)
    mixed_heads, lse_rows = attend(qkv, segs, vectors, far)
    mixed_stack = mixed_heads.reshape(pieces, -1, head_cols)
    mixed = exchange_axis(lambda j: block_at(mixed_stack, j), "ctx")
    mixed = jnp.transpose(mixed, (1, 0, 2)).reshape(rows * parts, -1)
    attn_part = mm_nt(mixed, w_out).reshape(parts, rows, width)
    attn_own = scatter_sum_axis(lambda j: block_at(attn_part, j), "tensor")

    x_own = layer_input.astype(f32)
    scale_one = inverse_scale(x_own)
    unit_one = x_own * scale_one
    hidden = x_own + attn_own
    scale_two = inverse_scale(hidden)
    unit_two = hidden * scale_two
    normed_two = (unit_two * gain_two).astype(bf16)

    normed_two_seq = gather_tokens(normed_two)
    units = w_down.shape[1]
    gate_up = mm(normed_two_seq, w_gu)
    gate, upper = gate_up[:, :units], gate_up[:, units:]
    inner_grad = mm(dy_seq, w_down)
    inner, gelu_pull = jax.vjp(lambda g, u: jax.nn.gelu(g, approximate=True) * u, gate, upper)
    inner = inner.astype(bf16)
    gate_grad, upper_grad = gelu_pull(inner_grad)
    gate_up_grad = jnp.concatenate([gate_grad.astype(bf16), upper_grad.astype(bf16)], axis=1)
    normed_two_part = mm_nt(gate_up_grad, w_gu).astype(bf16)
    normed_two_grad = scatter_tokens(normed_two_part)
    ff_part = mm_nt(inner, w_down).astype(bf16)
    ff_own = scatter_tokens(ff_part)
    block_output = (hidden + ff_own).astype(bf16)
    gate_out, up_out = scatter_weight(mm_tn(normed_two_seq, gate_up_grad), (units, units))
    (down_out,) = scatter_weight(mm_tn(dy_seq, inner), (units,))

    ff_gain_share = jnp.sum(normed_two_grad * unit_two, axis=0)
    hidden_grad = cotangent.astype(f32) + root_mean_square_backward(
        normed_two_grad, unit_two, scale_two, gain_two
    )
    attn_step = gather_axis(hidden_grad.astype(bf16), "tensor").reshape(rows * parts, width)
    mixed_grad = mm(attn_step, w_out).astype(bf16).reshape(rows * parts, pieces, head_cols)
    mixed_grad = exchange_axis(
        lambda j: lax.dynamic_index_in_dim(mixed_grad, j, 1, keepdims=False), "ctx"
    ).reshape(seq_len, head_cols)
    output_wgrad = mm_tn(attn_step, mixed)
    output_stack = output_wgrad.reshape(dps, -1, output_wgrad.shape[1])
    output_sum = scatter_sum_axis(lambda j: block_at(output_stack, j), "dp")
    output_sum = output_sum.reshape(pieces, -1, output_wgrad.shape[1])
    output_out = scatter_sum_axis(lambda j: block_at(output_sum, j), "ctx").T

    dq, dk, dv, diagonals, far_sums = attend_back(qkv, mixed_grad, segs, vectors, far, lse_rows)
    dqkv = jnp.concatenate([dq, dk, dv], axis=1)
    normed_one_part = mm_nt(dqkv, w_qkv).astype(bf16)
    normed_one_grad = scatter_tokens(normed_one_part)
    query_out, key_out, value_out = scatter_weight(
        mm_tn(normed_seq, dqkv), (head_cols, head_cols, head_cols)
    )
    attn_gain_share = jnp.sum(normed_one_grad * unit_one, axis=0)
    input_grads = (
        hidden_grad + root_mean_square_backward(normed_one_grad, unit_one, scale_one, gain_one)
    ).astype(bf16)

    far_total = jnp.sum(far_sums.reshape(heads, 2, TQ), axis=2)
    bias_own = jnp.dot(diagonals.reshape(heads, WIDE), lanes_onehot, precision=highest)
    bucket = jnp.arange(NB, dtype=jnp.int32)[None, :]
    bias_own = bias_own + jnp.where(bucket == NB // 2 - 1, far_total[:, 0:1], 0.0)
    bias_own = bias_own + jnp.where(bucket == NB - 1, far_total[:, 1:2], 0.0)
    bias_full = lax.dynamic_update_slice(
        jnp.zeros((NB, part_heads * parts), f32), bias_own.T, (jnp.int32(0), t * part_heads + z * heads)
    )
    own_segments = lax.dynamic_slice_in_dim(segments, t * rows, rows)
    valid = (own_segments != 0).astype(f32)
    out_values = block_output.astype(f32)
    grad_values = input_grads.astype(f32)
    local_sums = jnp.stack(
        [
            jnp.sum(valid * jnp.sum(out_values * out_values, axis=1)),
            jnp.sum(valid * jnp.sum(grad_values * grad_values, axis=1)),
            jnp.sum(valid),
        ]
    )
    gain_one_total, gain_two_total, bias_total, sums_total = lax.psum(
        (attn_gain_share, ff_gain_share, bias_full, local_sums), ("dp", "ctx", "tensor")
    )
    rms_stats = jnp.sqrt(sums_total[:2] / (sums_total[2] * width))
    return (
        block_output,
        input_grads,
        gain_one_total,
        query_out,
        key_out,
        value_out,
        output_out,
        bias_total,
        gain_two_total,
        gate_out,
        up_out,
        down_out.T,
        rms_stats,
    )


def solution(mesh):
    return jax.shard_map(
        shards,
        mesh=mesh,
        in_specs=(
            P(("dp", "ctx", "tensor"), None),
            P(("dp", "ctx")),
            P(("dp", "ctx")),
            P(("dp", "ctx"), "tensor"),
            P(("dp", "ctx"), "tensor"),
            P(("dp", "ctx"), "tensor"),
            P("tensor", ("dp", "ctx")),
            P(None, "tensor"),
            P(("dp", "ctx")),
            P(("dp", "ctx"), "tensor"),
            P(("dp", "ctx"), "tensor"),
            P("tensor", ("dp", "ctx")),
            P(("dp", "ctx", "tensor"), None),
        ),
        out_specs=(
            P(("dp", "ctx", "tensor"), None),
            P(("dp", "ctx", "tensor"), None),
            P(),
            P(("dp", "ctx"), "tensor"),
            P(("dp", "ctx"), "tensor"),
            P(("dp", "ctx"), "tensor"),
            P("tensor", ("dp", "ctx")),
            P(),
            P(),
            P(("dp", "ctx"), "tensor"),
            P(("dp", "ctx"), "tensor"),
            P("tensor", ("dp", "ctx")),
            P(),
        ),
        check_vma=False,
    )
```

```python
import functools

import jax
import jax.numpy as jnp
from jax import lax
from jax.experimental import pallas as pl
from jax.experimental.pallas import tpu as pltpu
from jax.sharding import PartitionSpec as P

NB = 32
DH = 64
edge_list = (12, 16, 23, 32, 46, 64, 91)
exact_span = 8
eps = 1e-06
highest = lax.Precision.HIGHEST
bf16 = jnp.bfloat16
f32 = jnp.float32

TQ = 256
BLOCK = 128
CORES = 2
REACH = 128
SPAN = TQ + 2 * REACH
WIDE = 1024


def bucket_of(relative):
    distance = jnp.abs(relative)
    coarse = jnp.full_like(distance, exact_span)
    for edge in edge_list:
        coarse = coarse + (distance >= edge).astype(jnp.int32)
    nearby = jnp.where(distance < exact_span, distance, coarse)
    return nearby + jnp.where(relative > 0, NB // 2, 0)


def lane_buckets():
    lane = jnp.arange(WIDE, dtype=jnp.int32)
    ahead = jnp.where(lane < TQ, lane, lane - WIDE)
    onehot = bucket_of(-ahead - REACH)[:, None] == jnp.arange(NB, dtype=jnp.int32)[None, :]
    return onehot.astype(f32)


def dot_nt(a, b):
    return lax.dot_general(a, b, (((1,), (1,)), ((), ())), preferred_element_type=f32)


def dot_nn(a, b):
    return lax.dot_general(a, b, (((1,), (0,)), ((), ())), preferred_element_type=f32)


def tile_range(tile, seq_len):
    start = tile * TQ
    low, high = max(0, start - REACH), min(seq_len, start + TQ + REACH)
    return start, low, high, low - (start - REACH), high - (start - REACH)


def tile_scores(key, query, strip_ref, far, seg_col, seg_row, tile, seq_len):
    start, low, high, strip_low, strip_high = tile_range(tile, seq_len)
    scores = dot_nt(key, query)
    parts = []
    if low > 0:
        parts.append(scores[:low] + far[0])
    parts.append(scores[low:high] + strip_ref[strip_low:strip_high])
    if high < seq_len:
        parts.append(scores[high:] + far[1])
    scores = jnp.concatenate(parts, axis=0) if len(parts) > 1 else parts[0]
    return jnp.where(seg_col == seg_row[:, start : start + TQ], scores, -1e30)


def make_strip(strip_ref, vector):
    tall = jnp.broadcast_to(vector, (SPAN, WIDE))
    strip_ref[...] = pltpu.roll(tall, 0, 1, stride=1, stride_axis=0)[:, :TQ]


def fold_diagonals(acc_ref):
    rest = jnp.zeros((8, WIDE - TQ), f32)
    groups = jnp.zeros((8, WIDE), f32)
    for at in range(0, SPAN, 8):
        wide = jnp.concatenate([acc_ref[at : at + 8, :], rest], axis=1)
        groups = groups + pltpu.roll(wide, (WIDE - at) % WIDE, 1)
    diagonals = groups[0:1]
    for row in range(1, 8):
        diagonals = diagonals + pltpu.roll(groups[row : row + 1], WIDE - row, 1)
    return diagonals


def core_major(block, here, seq_len):
    core = lax.rem(block % CORES + CORES - here, CORES)
    return pl.ds(pl.multiple_of((core * (seq_len // BLOCK // CORES) + block // CORES) * BLOCK, BLOCK), BLOCK)


def piece_major(block, here):
    core = lax.rem(block % CORES + CORES - here, CORES)
    return pl.ds(pl.multiple_of((block // CORES * CORES + core) * BLOCK, BLOCK), BLOCK)


def attend_kernel(
    seq_len,
    here_ref,
    q_in,
    k_in,
    v_in,
    segc_ref,
    segr_ref,
    vec_ref,
    far_ref,
    mix_out,
    lse_ref,
    strip_ref,
    q_ref,
    k_ref,
    v_ref,
    mix_ref,
):
    seg_col = segc_ref[...]
    seg_row = segr_ref[...]
    pair = pl.program_id(0)
    here = here_ref[0]
    for block in range(seq_len // BLOCK):
        rows = slice(block * BLOCK, (block + 1) * BLOCK)
        source = core_major(block, here, seq_len)
        q_ref[rows], k_ref[rows], v_ref[rows] = q_in[source], k_in[source], v_in[source]
    value_t = v_ref[...].T
    for half in range(2):
        make_strip(strip_ref, vec_ref[0, half : half + 1, :])
        far = (far_ref[2 * pair + half, 0], far_ref[2 * pair + half, 1])
        lanes = slice(half * DH, (half + 1) * DH)
        key = k_ref[:, lanes]
        for tile in range(seq_len // TQ):
            rows = slice(tile * TQ, (tile + 1) * TQ)
            query = q_ref[rows, lanes]
            scores = tile_scores(key, query, strip_ref, far, seg_col, seg_row, tile, seq_len)
            top = jnp.max(scores, axis=0, keepdims=True)
            expo = jnp.exp(scores - top)
            total = jnp.sum(expo, axis=0, keepdims=True)
            mixed_t = dot_nn(value_t[lanes, :], expo.astype(bf16)) * (1.0 / total)
            mix_ref[rows, lanes] = mixed_t.T.astype(bf16)
            lse_ref[0, half : half + 1, rows] = top + jnp.log(total)
    for block in range(seq_len // BLOCK):
        mix_out[piece_major(block, here)] = mix_ref[block * BLOCK : (block + 1) * BLOCK]


def attend_back_kernel(
    seq_len,
    here_ref,
    q_in,
    k_in,
    v_in,
    do_in,
    segc_ref,
    segr_ref,
    vec_ref,
    far_ref,
    lse_ref,
    dqkv_out,
    diag_ref,
    farsum_ref,
    strip_ref,
    acc_ref,
    dk_acc,
    dv_acc,
    q_ref,
    k_ref,
    v_ref,
    do_ref,
    dq_ref,
    dk_ref,
    dv_ref,
):
    seg_col = segc_ref[...]
    seg_row = segr_ref[...]
    pair = pl.program_id(0)
    here = here_ref[0]
    for block in range(seq_len // BLOCK):
        rows = slice(block * BLOCK, (block + 1) * BLOCK)
        source = core_major(block, here, seq_len)
        q_ref[rows], k_ref[rows], v_ref[rows] = q_in[source], k_in[source], v_in[source]
        do_ref[rows] = do_in[piece_major(block, here)]
    key_t = k_ref[...].T
    for half in range(2):
        make_strip(strip_ref, vec_ref[0, half : half + 1, :])
        far = (far_ref[2 * pair + half, 0], far_ref[2 * pair + half, 1])
        lanes = slice(half * DH, (half + 1) * DH)
        key = k_ref[:, lanes]
        value = v_ref[:, lanes]
        acc_ref[...] = jnp.zeros_like(acc_ref)
        far_before = jnp.zeros((1, TQ), f32)
        far_after = jnp.zeros((1, TQ), f32)
        for tile in range(seq_len // TQ):
            start, low, high, strip_low, strip_high = tile_range(tile, seq_len)
            rows = slice(start, start + TQ)
            query = q_ref[rows, lanes]
            mixed_grad = do_ref[rows, lanes]
            scores = tile_scores(key, query, strip_ref, far, seg_col, seg_row, tile, seq_len)
            probs = jnp.exp(scores - lse_ref[0, half : half + 1, rows])
            prob_grad = dot_nt(value, mixed_grad)
            centre = jnp.sum(probs * prob_grad, axis=0, keepdims=True)
            score_grad = probs * (prob_grad - centre)
            rounded = score_grad.astype(bf16)
            value_g = dot_nn(probs.astype(bf16), mixed_grad)
            key_g = dot_nn(rounded, query)
            if tile == 0:
                dv_acc[...] = value_g
                dk_acc[...] = key_g
            else:
                dv_acc[...] += value_g
                dk_acc[...] += key_g
            dq_ref[rows, lanes] = dot_nn(key_t[lanes, :], rounded).T.astype(bf16)
            acc_ref[strip_low:strip_high, :] += score_grad[low:high]
            if low > 0:
                far_before = far_before + jnp.sum(score_grad[:low], axis=0, keepdims=True)
            if high < seq_len:
                far_after = far_after + jnp.sum(score_grad[high:], axis=0, keepdims=True)
        dk_ref[:, lanes] = dk_acc[...].astype(bf16)
        dv_ref[:, lanes] = dv_acc[...].astype(bf16)
        diag_ref[0, half : half + 1, :] = fold_diagonals(acc_ref)
        farsum_ref[0, half : half + 1, 0:TQ] = far_before
        farsum_ref[0, half : half + 1, TQ : 2 * TQ] = far_after
    for block in range(seq_len // BLOCK):
        rows = slice(block * BLOCK, (block + 1) * BLOCK)
        target = core_major(block, here, seq_len)
        for at, ref in enumerate((dq_ref, dk_ref, dv_ref)):
            start = (at * pl.num_programs(0) + pair) * (2 * DH)
            dqkv_out[target, pl.ds(pl.multiple_of(start, 2 * DH), 2 * DH)] = ref[rows]


def kernel_params():
    return pltpu.CompilerParams(vmem_limit_bytes=56 * 1024 * 1024)


def attention_specs(seq_len, pairs):
    wide = lambda at: pl.BlockSpec((seq_len, 2 * DH), lambda p, at=at: (0, at * pairs + p))
    seg_c = pl.BlockSpec((seq_len, 1), lambda p: (0, 0))
    seg_r = pl.BlockSpec((1, seq_len), lambda p: (0, 0))
    vec = pl.BlockSpec((1, 2, WIDE), lambda p: (p, 0, 0))
    far = pl.BlockSpec(memory_space=pltpu.SMEM)
    lse = pl.BlockSpec((1, 2, seq_len), lambda p: (p, 0, 0))
    return wide, seg_c, seg_r, vec, far, lse


def attend(here, qkv, segs, vectors, far):
    seq_len = qkv.shape[0]
    pairs = vectors.shape[0]
    wide, seg_c, seg_r, vec, far_spec, lse = attention_specs(seq_len, pairs)
    work = pairs * 2 * seq_len * seq_len
    return pl.pallas_call(
        functools.partial(attend_kernel, seq_len),
        grid=(pairs,),
        in_specs=[far_spec, wide(0), wide(1), wide(2), seg_c, seg_r, vec, far_spec],
        out_specs=[wide(0), lse],
        out_shape=[
            jax.ShapeDtypeStruct((seq_len, pairs * 2 * DH), bf16),
            jax.ShapeDtypeStruct((pairs, 2, seq_len), f32),
        ],
        scratch_shapes=[pltpu.VMEM((SPAN, TQ), f32)] + [pltpu.VMEM((seq_len, 2 * DH), bf16)] * 4,
        compiler_params=kernel_params(),
        cost_estimate=pl.CostEstimate(
            flops=16 * DH * work, bytes_accessed=8 * seq_len * pairs * DH, transcendentals=work
        ),
        name="attend",
    )(here, qkv, qkv, qkv, segs[:, None], segs[None, :], vectors, far)


def attend_back(here, qkv, mixed_grad, segs, vectors, far, lse_rows):
    seq_len = qkv.shape[0]
    pairs = vectors.shape[0]
    wide, seg_c, seg_r, vec, far_spec, lse = attention_specs(seq_len, pairs)
    work = pairs * 2 * seq_len * seq_len
    dqkv_shape = (seq_len, pairs * 6 * DH)
    return pl.pallas_call(
        functools.partial(attend_back_kernel, seq_len),
        grid=(pairs,),
        in_specs=[far_spec, wide(0), wide(1), wide(2), wide(0), seg_c, seg_r, vec, far_spec, lse],
        out_specs=[
            pl.BlockSpec(dqkv_shape, lambda p: (0, 0)),
            vec,
            pl.BlockSpec((1, 2, 2 * TQ), lambda p: (p, 0, 0)),
        ],
        out_shape=[
            jax.ShapeDtypeStruct(dqkv_shape, bf16),
            jax.ShapeDtypeStruct((pairs, 2, WIDE), f32),
            jax.ShapeDtypeStruct((pairs, 2, 2 * TQ), f32),
        ],
        scratch_shapes=[
            pltpu.VMEM((SPAN, TQ), f32),
            pltpu.VMEM((SPAN, TQ), f32),
            pltpu.VMEM((seq_len, DH), f32),
            pltpu.VMEM((seq_len, DH), f32),
        ]
        + [pltpu.VMEM((seq_len, 2 * DH), bf16)] * 7,
        compiler_params=kernel_params(),
        cost_estimate=pl.CostEstimate(
            flops=40 * DH * work, bytes_accessed=16 * seq_len * pairs * DH, transcendentals=work
        ),
        name="attend_back",
    )(here, qkv, qkv, qkv, mixed_grad, segs[:, None], segs[None, :], vectors, far, lse_rows)


def shift(value, axis, by):
    size = lax.axis_size(axis)
    return lax.ppermute(value, axis, [(i, (i + by) % size) for i in range(size)])


def block_at(stack, at):
    return lax.dynamic_index_in_dim(stack, at, 0, keepdims=False)


def place(stack, block, at):
    return lax.dynamic_update_slice(stack, block[None], (at,) + (jnp.int32(0),) * block.ndim)


def arrivals(block, axis):
    return [shift(block, axis, k) for k in range(1, lax.axis_size(axis))]


def assemble(block, arrived, axis):
    size, me = lax.axis_size(axis), lax.axis_index(axis)
    stack = place(jnp.zeros((size,) + block.shape, block.dtype), block, me)
    for k in range(1, size):
        stack = place(stack, arrived[k - 1], (me - k) % size)
    return stack


def gather_axis(block, axis):
    return assemble(block, arrivals(block, axis), axis)


def flip(value, mask):
    size = lax.axis_size("dp")
    return lax.ppermute(value, "dp", [(i, i ^ mask) for i in range(size)])


def gather_rows(block):
    if lax.axis_size("dp") != 4:
        return flat(gather_axis(block, "dp"))
    me, half = lax.axis_index("dp"), block.shape[0] // 2
    near, other = flip(block, 1), flip(block, 2)
    first, second = flip(near[:half], 2), flip(other[half:], 1)
    stack = place(jnp.zeros((4,) + block.shape, block.dtype), block, me)
    stack = place(place(stack, near, me ^ 1), other, me ^ 2)
    zero = jnp.int32(0)
    stack = lax.dynamic_update_slice(stack, first[None], (me ^ 3, zero, zero))
    stack = lax.dynamic_update_slice(stack, second[None], (me ^ 3, jnp.int32(half), zero))
    return flat(stack)


def exchange_axis(block_of, axis):
    size, me = lax.axis_size(axis), lax.axis_index(axis)
    own = block_of(me)
    stack = place(jnp.zeros((size,) + own.shape, own.dtype), own, me)
    for k in range(1, size):
        stack = place(stack, shift(block_of((me + k) % size), axis, k), (me - k) % size)
    return stack


def scatter_sum_axis(block_of, axis):
    size, me = lax.axis_size(axis), lax.axis_index(axis)
    arrived = [shift(block_of((me + k) % size).astype(bf16), axis, k) for k in range(1, size)]
    total = block_of(me).astype(f32)
    for block in arrived:
        total = total + block.astype(f32)
    return total


def tie(value, *others):
    return lax.optimization_barrier((value,) + others)[0]


def swap(block):
    return shift(block, "tensor", 1)


def exchange(stack, axis):
    return lax.all_to_all(stack, axis, 0, 0)


def gather_bcast(rows, axis):
    return exchange(jnp.broadcast_to(rows[None], (lax.axis_size(axis),) + rows.shape), axis)


def gather_tokens(rows, axis):
    return both_cores(gather_bcast(rows, axis))


def both_cores(stack):
    return jnp.concatenate([stack, swap(stack)], axis=0).reshape(-1, stack.shape[-1])


def sum_of_cores(partial, axis):
    stack = partial.reshape(CORES, lax.axis_size(axis), -1, partial.shape[-1])
    return (stack[0].astype(f32) + swap(stack[1].astype(bf16)).astype(f32)).astype(bf16)


def sum_of_axis(stack, axis):
    return jnp.sum(exchange(stack, axis).astype(f32), axis=0)


def columns_in(matrix, order):
    wide = matrix.shape[1] // len(order)
    return jnp.concatenate([matrix[:, j * wide : (j + 1) * wide] for j in order], axis=1)


def by_piece(matrix):
    dps, pieces = lax.axis_size("dp"), lax.axis_size("ctx")
    return columns_in(matrix, [j * pieces + i for i in range(pieces) for j in range(dps)])


def by_dp(matrix):
    dps, pieces = lax.axis_size("dp"), lax.axis_size("ctx")
    return columns_in(matrix, [i * dps + j for j in range(dps) for i in range(pieces)])


def piece_columns(weights):
    pieces = lax.axis_size("ctx")
    split = [jnp.transpose(w.reshape(w.shape[0], pieces, -1), (1, 0, 2)) for w in weights]
    return jnp.concatenate(split, axis=2)


def own_rows(stack, widths):
    outs, at = [], 0
    for width in widths:
        part = stack[:, :, at : at + width].astype(f32)
        outs.append(jnp.transpose(part, (1, 0, 2)).reshape(part.shape[1], -1))
        at += width
    return outs


def send_weight(left, right):
    size, me = lax.axis_size("dp"), lax.axis_index("dp")
    wide = left.shape[1] // size

    def block_of(j):
        return mm_tn(lax.dynamic_slice_in_dim(left, j * wide, wide, 1), right)

    arrived = [shift(block_of((me + k) % size).astype(bf16), "dp", k) for k in range(1, size)]
    return block_of(me), arrived


def sum_weight(own, arrived):
    for block in arrived:
        own = own + block.astype(f32)
    return own.astype(bf16).reshape(lax.axis_size("ctx"), -1, own.shape[1])


def reduce_weight(left, right):
    if lax.axis_size("dp") != 4:
        own, arrived = send_weight(left, right)
        return sum_weight(own, arrived), arrived
    me, wide, half = lax.axis_index("dp"), left.shape[1] // 4, right.shape[1] // 2

    def block_of(j):
        return mm_tn(lax.dynamic_slice_in_dim(left, j * wide, wide, 1), right)

    far = block_of(me ^ 3).astype(bf16)
    near = block_of(me ^ 1).astype(bf16)
    other = block_of(me ^ 2).astype(bf16)
    from_near = flip(jnp.stack([near[:, :half], far[:, :half]]), 1)
    from_other = flip(jnp.stack([other[:, half:], far[:, half:]]), 2)
    own = block_of(me)
    low = flip((other[:, :half].astype(f32) + from_near[1].astype(f32)).astype(bf16), 2)
    high = flip((near[:, half:].astype(f32) + from_other[1].astype(f32)).astype(bf16), 1)
    low = own[:, :half] + from_near[0].astype(f32) + low.astype(f32)
    high = own[:, half:] + from_other[0].astype(f32) + high.astype(f32)
    return sum_weight(jnp.concatenate([low, high], axis=1), []), [from_near, from_other]


def flat(stack):
    return stack.reshape(-1, stack.shape[-1])


def root_mean_square_backward(grad, normalized, scale, gain):
    scaled = grad * gain
    return scale * (scaled - normalized * jnp.mean(scaled * normalized, axis=-1, keepdims=True))


def mm(a, b):
    return jnp.dot(a, b, preferred_element_type=f32)


def mm_nt(a, b):
    return dot_nt(a, b)


def mm_tn(a, b):
    return lax.dot_general(a, b, (((0,), (0,)), ((), ())), preferred_element_type=f32)


def inverse_scale(values):
    return lax.rsqrt(jnp.mean(values * values, axis=1, keepdims=True) + eps)


def shards(
    layer_input,
    segments,
    attn_gain,
    query_weight,
    key_weight,
    value_weight,
    output_weight,
    bias_table,
    ff_gain,
    gate_weight,
    up_weight,
    down_weight,
    cotangent,
):
    parts, pieces, dps = lax.axis_size("tensor"), lax.axis_size("ctx"), lax.axis_size("dp")
    t, z, s = lax.axis_index("tensor"), lax.axis_index("ctx"), lax.axis_index("dp")
    rows, width = layer_input.shape
    seq_len = rows * parts * pieces
    part_heads = bias_table.shape[1]
    heads = part_heads // pieces
    head_cols = heads * DH


    here = jnp.reshape(t, (1,)).astype(jnp.int32)

    small_in = jnp.concatenate([attn_gain, ff_gain, segments.astype(bf16)]).reshape(1, -1)
    small_pieces = gather_axis(small_in, "ctx").reshape(pieces, -1)
    gain_cols = attn_gain.shape[0]
    segs = small_pieces[:, 2 * gain_cols :].astype(jnp.int32).reshape(seq_len)
    gains = gather_axis(small_pieces[:, : 2 * gain_cols], "dp").reshape(dps, pieces, 2, gain_cols)
    gains = jnp.transpose(gains, (2, 0, 1, 3)).reshape(2, width).astype(f32)
    gain_one, gain_two = gains[0:1], gains[1:2]
    attn_blocks = piece_columns([query_weight, key_weight, value_weight])
    out_block = jnp.broadcast_to(output_weight.T[None], (pieces, output_weight.shape[1], part_heads * DH))
    attn_blocks = jnp.concatenate([attn_blocks, out_block], axis=2)
    attn_pieces = flat(exchange(tie(attn_blocks, small_pieces), "ctx"))

    units = down_weight.shape[0] // dps
    ff_weights = (gate_weight, up_weight, down_weight.T)
    ff_weights = lax.optimization_barrier(ff_weights + (small_pieces,))[:3]

    def ff_block(j):
        columns = [lax.dynamic_slice_in_dim(w, j * units, units, 1) for w in ff_weights]
        return jnp.concatenate(columns, axis=1)

    ff_arrived = [shift(ff_block((s + k) % dps), "dp", k) for k in range(1, dps)]
    x_copies = jnp.broadcast_to(layer_input[None], (pieces,) + layer_input.shape)
    x_core = exchange(tie(x_copies, attn_pieces, gains, *ff_arrived), "ctx")
    ff_rows = assemble(ff_block(s), ff_arrived, "dp")
    w_ff = lax.all_gather(flat(ff_rows), "ctx", axis=0, tiled=True)
    w_gu, w_down = w_ff[:, : 2 * units], w_ff[:, 2 * units :]

    w_qkv = gather_rows(attn_pieces[:, : 3 * head_cols])
    w_out = gather_rows(tie(attn_pieces, w_qkv)[:, 3 * head_cols :])
    x_seq = both_cores(tie(x_core, w_out))

    own_table = lax.dynamic_slice_in_dim(bias_table, z * heads, heads, 1)
    lanes_onehot = lane_buckets()
    vectors = jnp.dot(lanes_onehot, own_table, precision=highest).T.reshape(heads // 2, 2, WIDE)
    far = jnp.stack([own_table[NB // 2 - 1], own_table[NB - 1]], axis=1)

    x_wide = tie(x_seq, w_qkv).astype(f32)
    normed_seq = (x_wide * inverse_scale(x_wide) * gain_one).astype(bf16)
    qkv = mm(normed_seq, w_qkv).astype(bf16)
    dy_arrived = arrivals(tie(by_piece(cotangent), qkv), "dp")
    mixed_heads, lse_rows = attend(here, qkv, segs, vectors, far)
    mixed = exchange(
        tie(mixed_heads, *dy_arrived).reshape(pieces, parts * rows, head_cols), "ctx"
    )
    dy_all = both_cores(assemble(by_piece(cotangent), dy_arrived, "dp"))
    mixed = jnp.transpose(mixed, (1, 0, 2)).reshape(rows * parts, -1)
    attn_part = mm_nt(mixed, w_out)
    attn_own = attn_part[:rows] + swap(attn_part[rows:].astype(bf16)).astype(f32)

    x_own = layer_input.astype(f32)
    scale_one = inverse_scale(x_own)
    unit_one = x_own * scale_one
    hidden = x_own + attn_own
    scale_two = inverse_scale(hidden)
    unit_two = hidden * scale_two
    normed_two = (unit_two * gain_two).astype(bf16)

    normed_two_all = gather_tokens(tie(by_piece(normed_two), dy_all), "dp")
    gate_up = mm(normed_two_all, w_gu)
    inner_grad = mm(dy_all, w_down)
    gate, upper = gate_up[:, :units], gate_up[:, units:]
    inner, gelu_pull = jax.vjp(lambda g, u: jax.nn.gelu(g, approximate=True) * u, gate, upper)
    inner = inner.astype(bf16)
    gate_grad, upper_grad = gelu_pull(inner_grad)
    gate_up_grad = jnp.concatenate([gate_grad.astype(bf16), upper_grad.astype(bf16)], axis=1)
    normed_two_part = mm_nt(gate_up_grad, w_gu).astype(bf16)
    normed_two_core = sum_of_cores(normed_two_part, "dp")
    normed_two_sum = sum_of_axis(normed_two_core, "dp")
    gate_up_late, inner_late = lax.optimization_barrier(
        (gate_up_grad, inner, normed_two_core)
    )[:2]
    ff_wgrad = jnp.concatenate(
        [mm_tn(normed_two_all, gate_up_late).astype(bf16), mm_tn(dy_all, inner_late).astype(bf16)],
        axis=1,
    )
    ff_sum = lax.psum_scatter(ff_wgrad, "ctx", scatter_dimension=0, tiled=True)
    normed_two_sum = tie(normed_two_sum, ff_wgrad)
    normed_two_sum = by_dp(normed_two_sum)
    normed_two_grad = normed_two_sum

    ff_gain_share = jnp.sum(normed_two_grad * unit_two, axis=0)
    hidden_grad = cotangent.astype(f32) + root_mean_square_backward(
        normed_two_grad, unit_two, scale_two, gain_two
    )
    attn_step = hidden_grad.astype(bf16)
    attn_step = jnp.concatenate([attn_step, swap(attn_step)], axis=0)
    mixed_grad = mm(attn_step, w_out).astype(bf16).reshape(rows * parts, pieces, head_cols)
    mixed_grad = flat(exchange(jnp.transpose(mixed_grad, (1, 0, 2)), "ctx"))
    output_sum, output_arrived = reduce_weight(attn_step, mixed)
    ff_part = mm_nt(tie(inner_late, attn_step), w_down).astype(bf16)
    ff_core = sum_of_cores(ff_part, "dp")
    ff_stack = exchange(tie(ff_core, mixed_grad), "dp")

    mixed_grad = tie(mixed_grad, *output_arrived)
    dqkv, diagonals, far_sums = attend_back(
        here, qkv, mixed_grad, segs, vectors, far, lse_rows
    )
    dqkv = tie(dqkv, ff_stack, output_sum)
    normed_one_part = mm_nt(dqkv, w_qkv).astype(bf16)
    normed_one_core = sum_of_cores(normed_one_part, "ctx")
    normed_one_sum = sum_of_axis(normed_one_core, "ctx")
    ff_own = by_dp(jnp.sum(tie(ff_stack, normed_one_core).astype(f32), axis=0))
    block_output = (hidden + ff_own).astype(bf16)
    qkv_sum, _ = reduce_weight(normed_seq, tie(dqkv, normed_one_core))
    ff_blocks = tie(ff_sum, qkv_sum).reshape(dps, -1, 3 * units)
    ff_back = exchange_axis(lambda j: block_at(ff_blocks, j), "dp")
    gate_out, up_out, down_out = own_rows(ff_back, (units,) * 3)
    normed_one_grad = tie(normed_one_sum, block_output, ff_back)
    sums = jnp.concatenate([output_sum, qkv_sum], axis=2)
    back = exchange(tie(sums, normed_one_sum), "ctx")
    at = output_sum.shape[2]
    output_out = jnp.sum(back[:, :, :at].astype(f32), axis=0).T
    query_out, key_out, value_out = own_rows(back[:, :, at:], (head_cols,) * 3)
    attn_gain_share = jnp.sum(normed_one_grad * unit_one, axis=0)
    input_grads = (
        hidden_grad + root_mean_square_backward(normed_one_grad, unit_one, scale_one, gain_one)
    ).astype(bf16)

    far_total = jnp.sum(far_sums.reshape(heads, 2, TQ), axis=2)
    bias_own = jnp.dot(diagonals.reshape(heads, WIDE), lanes_onehot, precision=highest)
    bucket = jnp.arange(NB, dtype=jnp.int32)[None, :]
    bias_own = bias_own + jnp.where(bucket == NB // 2 - 1, far_total[:, 0:1], 0.0)
    bias_own = bias_own + jnp.where(bucket == NB - 1, far_total[:, 1:2], 0.0)
    bias_full = lax.dynamic_update_slice(
        jnp.zeros((NB, part_heads * parts), f32), bias_own.T, (jnp.int32(0), t * part_heads + z * heads)
    )
    own_segments = lax.dynamic_slice_in_dim(segments, t * rows, rows)
    valid = (own_segments != 0).astype(f32)
    out_values = block_output.astype(f32)
    grad_values = input_grads.astype(f32)
    local_sums = jnp.stack(
        [
            jnp.sum(valid * jnp.sum(out_values * out_values, axis=1)),
            jnp.sum(valid * jnp.sum(grad_values * grad_values, axis=1)),
            jnp.sum(valid),
        ]
    )
    small = jnp.concatenate(
        [attn_gain_share, ff_gain_share, bias_full.reshape(-1), jnp.pad(local_sums, (0, BLOCK - 3))]
    ).reshape(-1, BLOCK)
    for axis in ("tensor", "dp", "ctx"):
        small = jnp.sum(gather_axis(small, axis), axis=0)
    small = small.reshape(-1)
    gain_one_total, gain_two_total = small[:width], small[width : 2 * width]
    bias_total = small[2 * width : 2 * width + bias_full.size].reshape(bias_full.shape)
    sums_total = small[2 * width + bias_full.size :]
    rms_stats = jnp.sqrt(sums_total[:2] / (sums_total[2] * width))
    return (
        block_output,
        input_grads,
        gain_one_total,
        query_out,
        key_out,
        value_out,
        output_out,
        bias_total,
        gain_two_total,
        gate_out,
        up_out,
        down_out.T,
        rms_stats,
    )


def solution(mesh):
    return jax.shard_map(
        shards,
        mesh=mesh,
        in_specs=(
            P(("dp", "ctx", "tensor"), None),
            P(("dp", "ctx")),
            P(("dp", "ctx")),
            P(("dp", "ctx"), "tensor"),
            P(("dp", "ctx"), "tensor"),
            P(("dp", "ctx"), "tensor"),
            P("tensor", ("dp", "ctx")),
            P(None, "tensor"),
            P(("dp", "ctx")),
            P(("dp", "ctx"), "tensor"),
            P(("dp", "ctx"), "tensor"),
            P("tensor", ("dp", "ctx")),
            P(("dp", "ctx", "tensor"), None),
        ),
        out_specs=(
            P(("dp", "ctx", "tensor"), None),
            P(("dp", "ctx", "tensor"), None),
            P(),
            P(("dp", "ctx"), "tensor"),
            P(("dp", "ctx"), "tensor"),
            P(("dp", "ctx"), "tensor"),
            P("tensor", ("dp", "ctx")),
            P(),
            P(),
            P(("dp", "ctx"), "tensor"),
            P(("dp", "ctx"), "tensor"),
            P("tensor", ("dp", "ctx")),
            P(),
        ),
        check_vma=False,
    )
```

```python
import functools

import jax
import jax.numpy as jnp
from jax import lax
from jax.experimental import pallas as pl
from jax.experimental.pallas import tpu as pltpu
from jax.sharding import PartitionSpec as P

NB = 32
DH = 64
edge_list = (12, 16, 23, 32, 46, 64, 91)
exact_span = 8
eps = 1e-06
highest = lax.Precision.HIGHEST
bf16 = jnp.bfloat16
f32 = jnp.float32

TQ = 256
BLOCK = 128
CORES = 2
REACH = 128
SPAN = TQ + 2 * REACH
WIDE = 1024


def bucket_of(relative):
    distance = jnp.abs(relative)
    coarse = jnp.full_like(distance, exact_span)
    for edge in edge_list:
        coarse = coarse + (distance >= edge).astype(jnp.int32)
    nearby = jnp.where(distance < exact_span, distance, coarse)
    return nearby + jnp.where(relative > 0, NB // 2, 0)


def lane_buckets():
    lane = jnp.arange(WIDE, dtype=jnp.int32)
    ahead = jnp.where(lane < TQ, lane, lane - WIDE)
    onehot = bucket_of(-ahead - REACH)[:, None] == jnp.arange(NB, dtype=jnp.int32)[None, :]
    return onehot.astype(f32)


def dot_nt(a, b):
    return lax.dot_general(a, b, (((1,), (1,)), ((), ())), preferred_element_type=f32)


def dot_nn(a, b):
    return lax.dot_general(a, b, (((1,), (0,)), ((), ())), preferred_element_type=f32)


def tile_range(tile, seq_len):
    start = tile * TQ
    low, high = max(0, start - REACH), min(seq_len, start + TQ + REACH)
    return start, low, high, low - (start - REACH), high - (start - REACH)


def tile_scores(key, query, strip_ref, far, seg_col, seg_row, tile, seq_len):
    start, low, high, strip_low, strip_high = tile_range(tile, seq_len)
    scores = dot_nt(key, query)
    parts = []
    if low > 0:
        parts.append(scores[:low] + far[0])
    parts.append(scores[low:high] + strip_ref[strip_low:strip_high])
    if high < seq_len:
        parts.append(scores[high:] + far[1])
    scores = jnp.concatenate(parts, axis=0) if len(parts) > 1 else parts[0]
    return jnp.where(seg_col == seg_row[:, start : start + TQ], scores, -1e30)


def make_strip(strip_ref, vector):
    tall = jnp.broadcast_to(vector, (SPAN, WIDE))
    strip_ref[...] = pltpu.roll(tall, 0, 1, stride=1, stride_axis=0)[:, :TQ]


def fold_diagonals(acc_ref):
    rest = jnp.zeros((8, WIDE - TQ), f32)
    groups = jnp.zeros((8, WIDE), f32)
    for at in range(0, SPAN, 8):
        wide = jnp.concatenate([acc_ref[at : at + 8, :], rest], axis=1)
        groups = groups + pltpu.roll(wide, (WIDE - at) % WIDE, 1)
    diagonals = groups[0:1]
    for row in range(1, 8):
        diagonals = diagonals + pltpu.roll(groups[row : row + 1], WIDE - row, 1)
    return diagonals


def core_major(block, here, seq_len):
    core = lax.rem(block % CORES + CORES - here, CORES)
    return pl.ds(pl.multiple_of((core * (seq_len // BLOCK // CORES) + block // CORES) * BLOCK, BLOCK), BLOCK)


def piece_major(block, here):
    core = lax.rem(block % CORES + CORES - here, CORES)
    return pl.ds(pl.multiple_of((block // CORES * CORES + core) * BLOCK, BLOCK), BLOCK)


def attend_kernel(
    seq_len,
    here_ref,
    q_in,
    k_in,
    v_in,
    segc_ref,
    segr_ref,
    vec_ref,
    far_ref,
    mix_out,
    lse_ref,
    strip_ref,
    q_ref,
    k_ref,
    v_ref,
    mix_ref,
):
    seg_col = segc_ref[...]
    seg_row = segr_ref[...]
    pair = pl.program_id(0)
    here = here_ref[0]
    for block in range(seq_len // BLOCK):
        rows = slice(block * BLOCK, (block + 1) * BLOCK)
        source = core_major(block, here, seq_len)
        q_ref[rows], k_ref[rows], v_ref[rows] = q_in[source], k_in[source], v_in[source]
    value_t = v_ref[...].T
    for half in range(2):
        make_strip(strip_ref, vec_ref[0, half : half + 1, :])
        far = (far_ref[2 * pair + half, 0], far_ref[2 * pair + half, 1])
        lanes = slice(half * DH, (half + 1) * DH)
        key = k_ref[:, lanes]
        for tile in range(seq_len // TQ):
            rows = slice(tile * TQ, (tile + 1) * TQ)
            query = q_ref[rows, lanes]
            scores = tile_scores(key, query, strip_ref, far, seg_col, seg_row, tile, seq_len)
            top = jnp.max(scores, axis=0, keepdims=True)
            expo = jnp.exp(scores - top)
            total = jnp.sum(expo, axis=0, keepdims=True)
            mixed_t = dot_nn(value_t[lanes, :], expo.astype(bf16)) * (1.0 / total)
            mix_ref[rows, lanes] = mixed_t.T.astype(bf16)
            lse_ref[0, half : half + 1, rows] = top + jnp.log(total)
    for block in range(seq_len // BLOCK):
        mix_out[piece_major(block, here)] = mix_ref[block * BLOCK : (block + 1) * BLOCK]


def attend_back_kernel(
    seq_len,
    here_ref,
    q_in,
    k_in,
    v_in,
    do_in,
    segc_ref,
    segr_ref,
    vec_ref,
    far_ref,
    lse_ref,
    dqkv_out,
    diag_ref,
    farsum_ref,
    strip_ref,
    acc_ref,
    dk_acc,
    dv_acc,
    q_ref,
    k_ref,
    v_ref,
    do_ref,
    dq_ref,
    dk_ref,
    dv_ref,
):
    seg_col = segc_ref[...]
    seg_row = segr_ref[...]
    pair = pl.program_id(0)
    here = here_ref[0]
    for block in range(seq_len // BLOCK):
        rows = slice(block * BLOCK, (block + 1) * BLOCK)
        source = core_major(block, here, seq_len)
        q_ref[rows], k_ref[rows], v_ref[rows] = q_in[source], k_in[source], v_in[source]
        do_ref[rows] = do_in[piece_major(block, here)]
    key_t = k_ref[...].T
    for half in range(2):
        make_strip(strip_ref, vec_ref[0, half : half + 1, :])
        far = (far_ref[2 * pair + half, 0], far_ref[2 * pair + half, 1])
        lanes = slice(half * DH, (half + 1) * DH)
        key = k_ref[:, lanes]
        value = v_ref[:, lanes]
        acc_ref[...] = jnp.zeros_like(acc_ref)
        far_before = jnp.zeros((1, TQ), f32)
        far_after = jnp.zeros((1, TQ), f32)
        for tile in range(seq_len // TQ):
            start, low, high, strip_low, strip_high = tile_range(tile, seq_len)
            rows = slice(start, start + TQ)
            query = q_ref[rows, lanes]
            mixed_grad = do_ref[rows, lanes]
            scores = tile_scores(key, query, strip_ref, far, seg_col, seg_row, tile, seq_len)
            probs = jnp.exp(scores - lse_ref[0, half : half + 1, rows])
            prob_grad = dot_nt(value, mixed_grad)
            centre = jnp.sum(probs * prob_grad, axis=0, keepdims=True)
            score_grad = probs * (prob_grad - centre)
            rounded = score_grad.astype(bf16)
            value_g = dot_nn(probs.astype(bf16), mixed_grad)
            key_g = dot_nn(rounded, query)
            if tile == 0:
                dv_acc[...] = value_g
                dk_acc[...] = key_g
            else:
                dv_acc[...] += value_g
                dk_acc[...] += key_g
            dq_ref[rows, lanes] = dot_nn(key_t[lanes, :], rounded).T.astype(bf16)
            acc_ref[strip_low:strip_high, :] += score_grad[low:high]
            if low > 0:
                far_before = far_before + jnp.sum(score_grad[:low], axis=0, keepdims=True)
            if high < seq_len:
                far_after = far_after + jnp.sum(score_grad[high:], axis=0, keepdims=True)
        dk_ref[:, lanes] = dk_acc[...].astype(bf16)
        dv_ref[:, lanes] = dv_acc[...].astype(bf16)
        diag_ref[0, half : half + 1, :] = fold_diagonals(acc_ref)
        farsum_ref[0, half : half + 1, 0:TQ] = far_before
        farsum_ref[0, half : half + 1, TQ : 2 * TQ] = far_after
    for block in range(seq_len // BLOCK):
        rows = slice(block * BLOCK, (block + 1) * BLOCK)
        target = core_major(block, here, seq_len)
        for at, ref in enumerate((dq_ref, dk_ref, dv_ref)):
            start = (at * pl.num_programs(0) + pair) * (2 * DH)
            dqkv_out[target, pl.ds(pl.multiple_of(start, 2 * DH), 2 * DH)] = ref[rows]


def kernel_params():
    return pltpu.CompilerParams(vmem_limit_bytes=56 * 1024 * 1024)


def attention_specs(seq_len, pairs):
    wide = lambda at: pl.BlockSpec((seq_len, 2 * DH), lambda p, at=at: (0, at * pairs + p))
    seg_c = pl.BlockSpec((seq_len, 1), lambda p: (0, 0))
    seg_r = pl.BlockSpec((1, seq_len), lambda p: (0, 0))
    vec = pl.BlockSpec((1, 2, WIDE), lambda p: (p, 0, 0))
    far = pl.BlockSpec(memory_space=pltpu.SMEM)
    lse = pl.BlockSpec((1, 2, seq_len), lambda p: (p, 0, 0))
    return wide, seg_c, seg_r, vec, far, lse


def attend(here, qkv, segs, vectors, far):
    seq_len = qkv.shape[0]
    pairs = vectors.shape[0]
    wide, seg_c, seg_r, vec, far_spec, lse = attention_specs(seq_len, pairs)
    work = pairs * 2 * seq_len * seq_len
    return pl.pallas_call(
        functools.partial(attend_kernel, seq_len),
        grid=(pairs,),
        in_specs=[far_spec, wide(0), wide(1), wide(2), seg_c, seg_r, vec, far_spec],
        out_specs=[wide(0), lse],
        out_shape=[
            jax.ShapeDtypeStruct((seq_len, pairs * 2 * DH), bf16),
            jax.ShapeDtypeStruct((pairs, 2, seq_len), f32),
        ],
        scratch_shapes=[pltpu.VMEM((SPAN, TQ), f32)] + [pltpu.VMEM((seq_len, 2 * DH), bf16)] * 4,
        compiler_params=kernel_params(),
        cost_estimate=pl.CostEstimate(
            flops=16 * DH * work, bytes_accessed=8 * seq_len * pairs * DH, transcendentals=work
        ),
        name="attend",
    )(here, qkv, qkv, qkv, segs[:, None], segs[None, :], vectors, far)


def attend_back(here, qkv, mixed_grad, segs, vectors, far, lse_rows):
    seq_len = qkv.shape[0]
    pairs = vectors.shape[0]
    wide, seg_c, seg_r, vec, far_spec, lse = attention_specs(seq_len, pairs)
    work = pairs * 2 * seq_len * seq_len
    dqkv_shape = (seq_len, pairs * 6 * DH)
    return pl.pallas_call(
        functools.partial(attend_back_kernel, seq_len),
        grid=(pairs,),
        in_specs=[far_spec, wide(0), wide(1), wide(2), wide(0), seg_c, seg_r, vec, far_spec, lse],
        out_specs=[
            pl.BlockSpec(dqkv_shape, lambda p: (0, 0)),
            vec,
            pl.BlockSpec((1, 2, 2 * TQ), lambda p: (p, 0, 0)),
        ],
        out_shape=[
            jax.ShapeDtypeStruct(dqkv_shape, bf16),
            jax.ShapeDtypeStruct((pairs, 2, WIDE), f32),
            jax.ShapeDtypeStruct((pairs, 2, 2 * TQ), f32),
        ],
        scratch_shapes=[
            pltpu.VMEM((SPAN, TQ), f32),
            pltpu.VMEM((SPAN, TQ), f32),
            pltpu.VMEM((seq_len, DH), f32),
            pltpu.VMEM((seq_len, DH), f32),
        ]
        + [pltpu.VMEM((seq_len, 2 * DH), bf16)] * 7,
        compiler_params=kernel_params(),
        cost_estimate=pl.CostEstimate(
            flops=40 * DH * work, bytes_accessed=16 * seq_len * pairs * DH, transcendentals=work
        ),
        name="attend_back",
    )(here, qkv, qkv, qkv, mixed_grad, segs[:, None], segs[None, :], vectors, far, lse_rows)


def shift(value, axis, by):
    size = lax.axis_size(axis)
    return lax.ppermute(value, axis, [(i, (i + by) % size) for i in range(size)])


def block_at(stack, at):
    return lax.dynamic_index_in_dim(stack, at, 0, keepdims=False)


def place(stack, block, at):
    return lax.dynamic_update_slice(stack, block[None], (at,) + (jnp.int32(0),) * block.ndim)


def arrivals(block, axis):
    return [shift(block, axis, k) for k in range(1, lax.axis_size(axis))]


def assemble(block, arrived, axis):
    size, me = lax.axis_size(axis), lax.axis_index(axis)
    stack = place(jnp.zeros((size,) + block.shape, block.dtype), block, me)
    for k in range(1, size):
        stack = place(stack, arrived[k - 1], (me - k) % size)
    return stack


def gather_axis(block, axis):
    return assemble(block, arrivals(block, axis), axis)


def flip(value, mask):
    size = lax.axis_size("dp")
    return lax.ppermute(value, "dp", [(i, i ^ mask) for i in range(size)])


def gather_rows(block):
    if lax.axis_size("dp") != 4:
        return flat(gather_axis(block, "dp"))
    me, half = lax.axis_index("dp"), block.shape[0] // 2
    near, other = flip(block, 1), flip(block, 2)
    first, second = flip(near[:half], 2), flip(other[half:], 1)
    stack = place(jnp.zeros((4,) + block.shape, block.dtype), block, me)
    stack = place(place(stack, near, me ^ 1), other, me ^ 2)
    zero = jnp.int32(0)
    stack = lax.dynamic_update_slice(stack, first[None], (me ^ 3, zero, zero))
    stack = lax.dynamic_update_slice(stack, second[None], (me ^ 3, jnp.int32(half), zero))
    return flat(stack)


def exchange_axis(block_of, axis):
    size, me = lax.axis_size(axis), lax.axis_index(axis)
    own = block_of(me)
    stack = place(jnp.zeros((size,) + own.shape, own.dtype), own, me)
    for k in range(1, size):
        stack = place(stack, shift(block_of((me + k) % size), axis, k), (me - k) % size)
    return stack


def scatter_sum_axis(block_of, axis):
    size, me = lax.axis_size(axis), lax.axis_index(axis)
    arrived = [shift(block_of((me + k) % size).astype(bf16), axis, k) for k in range(1, size)]
    total = block_of(me).astype(f32)
    for block in arrived:
        total = total + block.astype(f32)
    return total


def tie(value, *others):
    return lax.optimization_barrier((value,) + others)[0]


def swap(block):
    return shift(block, "tensor", 1)


def exchange(stack, axis):
    return lax.all_to_all(stack, axis, 0, 0)


def gather_bcast(rows, axis):
    return exchange(jnp.broadcast_to(rows[None], (lax.axis_size(axis),) + rows.shape), axis)


def gather_tokens(rows, axis):
    return both_cores(gather_bcast(rows, axis))


def both_cores(stack):
    return jnp.concatenate([stack, swap(stack)], axis=0).reshape(-1, stack.shape[-1])


def sum_of_cores(partial, axis):
    stack = partial.reshape(CORES, lax.axis_size(axis), -1, partial.shape[-1])
    return (stack[0].astype(f32) + swap(stack[1].astype(bf16)).astype(f32)).astype(bf16)


def sum_of_axis(stack, axis):
    return jnp.sum(exchange(stack, axis).astype(f32), axis=0)


def columns_in(matrix, order):
    wide = matrix.shape[1] // len(order)
    return jnp.concatenate([matrix[:, j * wide : (j + 1) * wide] for j in order], axis=1)


def by_piece(matrix):
    dps, pieces = lax.axis_size("dp"), lax.axis_size("ctx")
    return columns_in(matrix, [j * pieces + i for i in range(pieces) for j in range(dps)])


def by_dp(matrix):
    dps, pieces = lax.axis_size("dp"), lax.axis_size("ctx")
    return columns_in(matrix, [i * dps + j for j in range(dps) for i in range(pieces)])


def piece_columns(weights):
    pieces = lax.axis_size("ctx")
    split = [jnp.transpose(w.reshape(w.shape[0], pieces, -1), (1, 0, 2)) for w in weights]
    return jnp.concatenate(split, axis=2)


def own_rows(stack, widths):
    outs, at = [], 0
    for width in widths:
        part = stack[:, :, at : at + width].astype(f32)
        outs.append(jnp.transpose(part, (1, 0, 2)).reshape(part.shape[1], -1))
        at += width
    return outs


def send_weight(left, right):
    size, me = lax.axis_size("dp"), lax.axis_index("dp")
    wide = left.shape[1] // size

    def block_of(j):
        return mm_tn(lax.dynamic_slice_in_dim(left, j * wide, wide, 1), right)

    arrived = [shift(block_of((me + k) % size).astype(bf16), "dp", k) for k in range(1, size)]
    return block_of(me), arrived


def sum_weight(own, arrived):
    for block in arrived:
        own = own + block.astype(f32)
    return own.astype(bf16).reshape(lax.axis_size("ctx"), -1, own.shape[1])


def reduce_weight(left, right):
    if lax.axis_size("dp") != 4:
        own, arrived = send_weight(left, right)
        return sum_weight(own, arrived), arrived
    me, wide, half = lax.axis_index("dp"), left.shape[1] // 4, right.shape[1] // 2

    def block_of(j):
        return mm_tn(lax.dynamic_slice_in_dim(left, j * wide, wide, 1), right)

    far = block_of(me ^ 3).astype(bf16)
    near = block_of(me ^ 1).astype(bf16)
    other = block_of(me ^ 2).astype(bf16)
    from_near = flip(jnp.stack([near[:, :half], far[:, :half]]), 1)
    from_other = flip(jnp.stack([other[:, half:], far[:, half:]]), 2)
    own = block_of(me)
    low = flip((other[:, :half].astype(f32) + from_near[1].astype(f32)).astype(bf16), 2)
    high = flip((near[:, half:].astype(f32) + from_other[1].astype(f32)).astype(bf16), 1)
    low = own[:, :half] + from_near[0].astype(f32) + low.astype(f32)
    high = own[:, half:] + from_other[0].astype(f32) + high.astype(f32)
    return sum_weight(jnp.concatenate([low, high], axis=1), []), [from_near, from_other]


def flat(stack):
    return stack.reshape(-1, stack.shape[-1])


def root_mean_square_backward(grad, normalized, scale, gain):
    scaled = grad * gain
    return scale * (scaled - normalized * jnp.mean(scaled * normalized, axis=-1, keepdims=True))


def mm(a, b):
    return jnp.dot(a, b, preferred_element_type=f32)


def mm_nt(a, b):
    return dot_nt(a, b)


def mm_tn(a, b):
    return lax.dot_general(a, b, (((0,), (0,)), ((), ())), preferred_element_type=f32)


def inverse_scale(values):
    return lax.rsqrt(jnp.mean(values * values, axis=1, keepdims=True) + eps)


def shards(
    layer_input,
    segments,
    attn_gain,
    query_weight,
    key_weight,
    value_weight,
    output_weight,
    bias_table,
    ff_gain,
    gate_weight,
    up_weight,
    down_weight,
    cotangent,
):
    parts, pieces, dps = lax.axis_size("tensor"), lax.axis_size("ctx"), lax.axis_size("dp")
    t, z, s = lax.axis_index("tensor"), lax.axis_index("ctx"), lax.axis_index("dp")
    rows, width = layer_input.shape
    seq_len = rows * parts * pieces
    part_heads = bias_table.shape[1]
    heads = part_heads // pieces
    head_cols = heads * DH


    here = jnp.reshape(t, (1,)).astype(jnp.int32)

    x_core = lax.all_gather(layer_input, "ctx", axis=0)
    small_in = jnp.concatenate([attn_gain, ff_gain, segments.astype(bf16)]).reshape(1, -1)
    small_pieces = gather_axis(small_in, "ctx").reshape(pieces, -1)
    gain_cols = attn_gain.shape[0]
    segs = small_pieces[:, 2 * gain_cols :].astype(jnp.int32).reshape(seq_len)
    attn_blocks = piece_columns([query_weight, key_weight, value_weight])
    out_block = jnp.broadcast_to(output_weight.T[None], (pieces, output_weight.shape[1], part_heads * DH))
    attn_blocks = jnp.concatenate([attn_blocks, out_block], axis=2)
    attn_pieces = flat(exchange(tie(attn_blocks, small_pieces), "ctx"))

    units = down_weight.shape[0] // dps
    ff_weights = (gate_weight, up_weight, down_weight.T)
    ff_weights = lax.optimization_barrier(ff_weights + (small_pieces,))[:3]

    def ff_block(j):
        columns = [lax.dynamic_slice_in_dim(w, j * units, units, 1) for w in ff_weights]
        return jnp.concatenate(columns, axis=1)

    ff_arrived = [shift(ff_block((s + k) % dps), "dp", k) for k in range(1, dps)]
    gains = gather_axis(tie(small_pieces, *ff_arrived)[:, : 2 * gain_cols], "dp")
    gains = gains.reshape(dps, pieces, 2, gain_cols)
    gains = jnp.transpose(gains, (2, 0, 1, 3)).reshape(2, width).astype(f32)
    gain_one, gain_two = gains[0:1], gains[1:2]
    dy_own = by_piece(cotangent)
    dy_arrived = arrivals(tie(dy_own, *ff_arrived), "dp")
    attn_pieces = tie(attn_pieces, gains, *ff_arrived, *dy_arrived)
    ff_rows = assemble(ff_block(s), ff_arrived, "dp")
    w_ff = lax.all_gather(flat(ff_rows), "ctx", axis=0, tiled=True)
    w_gu, w_down = w_ff[:, : 2 * units], w_ff[:, 2 * units :]

    w_qkv = gather_rows(attn_pieces[:, : 3 * head_cols])
    x_seq = both_cores(x_core)

    own_table = lax.dynamic_slice_in_dim(bias_table, z * heads, heads, 1)
    lanes_onehot = lane_buckets()
    vectors = jnp.dot(lanes_onehot, own_table, precision=highest).T.reshape(heads // 2, 2, WIDE)
    far = jnp.stack([own_table[NB // 2 - 1], own_table[NB - 1]], axis=1)

    x_wide = tie(x_seq, w_qkv).astype(f32)
    normed_seq = (x_wide * inverse_scale(x_wide) * gain_one).astype(bf16)
    qkv = mm(normed_seq, w_qkv).astype(bf16)
    w_out = gather_rows(tie(attn_pieces, qkv)[:, 3 * head_cols :])
    mixed_heads, lse_rows = attend(here, qkv, segs, vectors, far)
    mixed = exchange(mixed_heads.reshape(pieces, parts * rows, head_cols), "ctx")
    dy_all = both_cores(assemble(tie(dy_own, qkv), dy_arrived, "dp"))
    mixed = jnp.transpose(mixed, (1, 0, 2)).reshape(rows * parts, -1)
    attn_part = mm_nt(mixed, w_out)
    attn_own = attn_part[:rows] + swap(attn_part[rows:].astype(bf16)).astype(f32)

    x_own = layer_input.astype(f32)
    scale_one = inverse_scale(x_own)
    unit_one = x_own * scale_one
    hidden = x_own + attn_own
    scale_two = inverse_scale(hidden)
    unit_two = hidden * scale_two
    normed_two = (unit_two * gain_two).astype(bf16)

    normed_two_all = gather_tokens(tie(by_piece(normed_two), dy_all), "dp")
    gate_up = mm(normed_two_all, w_gu)
    inner_grad = mm(dy_all, w_down)
    gate, upper = gate_up[:, :units], gate_up[:, units:]
    inner, gelu_pull = jax.vjp(lambda g, u: jax.nn.gelu(g, approximate=True) * u, gate, upper)
    inner = inner.astype(bf16)
    gate_grad, upper_grad = gelu_pull(inner_grad)
    gate_up_grad = jnp.concatenate([gate_grad.astype(bf16), upper_grad.astype(bf16)], axis=1)
    normed_two_part = mm_nt(gate_up_grad, w_gu).astype(bf16)
    normed_two_core = sum_of_cores(normed_two_part, "dp")
    normed_two_sum = sum_of_axis(normed_two_core, "dp")
    gate_up_late, inner_late = lax.optimization_barrier(
        (gate_up_grad, inner, normed_two_core)
    )[:2]
    down_wgrad = mm_tn(dy_all, inner).astype(bf16)
    down_sum = lax.psum_scatter(down_wgrad, "ctx", scatter_dimension=0, tiled=True)
    gu_wgrad = mm_tn(normed_two_all, gate_up_late).astype(bf16)
    gu_sum = lax.psum_scatter(gu_wgrad, "ctx", scatter_dimension=0, tiled=True)
    normed_two_sum = tie(normed_two_sum, gu_wgrad)
    normed_two_sum = by_dp(normed_two_sum)
    normed_two_grad = normed_two_sum

    ff_gain_share = jnp.sum(normed_two_grad * unit_two, axis=0)
    hidden_grad = cotangent.astype(f32) + root_mean_square_backward(
        normed_two_grad, unit_two, scale_two, gain_two
    )
    attn_step = hidden_grad.astype(bf16)
    attn_step = jnp.concatenate([attn_step, swap(attn_step)], axis=0)
    mixed_grad = mm(attn_step, w_out).astype(bf16).reshape(rows * parts, pieces, head_cols)
    mixed_grad = flat(exchange(jnp.transpose(mixed_grad, (1, 0, 2)), "ctx"))
    output_sum, output_arrived = reduce_weight(attn_step, mixed)
    ff_part = mm_nt(tie(inner_late, attn_step), w_down).astype(bf16)
    ff_core = sum_of_cores(ff_part, "dp")
    ff_stack = exchange(tie(ff_core, mixed_grad), "dp")

    mixed_grad = tie(mixed_grad, down_sum, *output_arrived)
    dqkv, diagonals, far_sums = attend_back(
        here, qkv, mixed_grad, segs, vectors, far, lse_rows
    )
    dqkv = tie(dqkv, ff_stack, output_sum)
    normed_one_part = mm_nt(dqkv, w_qkv).astype(bf16)
    normed_one_core = sum_of_cores(normed_one_part, "ctx")
    normed_one_sum = sum_of_axis(normed_one_core, "ctx")
    ff_own = by_dp(jnp.sum(tie(ff_stack, normed_one_core).astype(f32), axis=0))
    block_output = (hidden + ff_own).astype(bf16)
    qkv_sum, _ = reduce_weight(normed_seq, tie(dqkv, normed_one_core))
    ff_blocks = jnp.concatenate([gu_sum, down_sum], axis=1)
    ff_blocks = tie(ff_blocks, qkv_sum).reshape(dps, -1, 3 * units)
    ff_back = exchange_axis(lambda j: block_at(ff_blocks, j), "dp")
    gate_out, up_out, down_out = own_rows(ff_back, (units,) * 3)
    down_out = down_out.T
    normed_one_grad = tie(normed_one_sum, block_output, ff_back)
    sums = jnp.concatenate([output_sum, qkv_sum], axis=2)
    back = exchange(tie(sums, normed_one_sum), "ctx")
    attn_gain_share = jnp.sum(normed_one_grad * unit_one, axis=0)
    input_grads = (
        hidden_grad + root_mean_square_backward(normed_one_grad, unit_one, scale_one, gain_one)
    ).astype(bf16)

    far_total = jnp.sum(far_sums.reshape(heads, 2, TQ), axis=2)
    bias_own = jnp.dot(diagonals.reshape(heads, WIDE), lanes_onehot, precision=highest)
    bucket = jnp.arange(NB, dtype=jnp.int32)[None, :]
    bias_own = bias_own + jnp.where(bucket == NB // 2 - 1, far_total[:, 0:1], 0.0)
    bias_own = bias_own + jnp.where(bucket == NB - 1, far_total[:, 1:2], 0.0)
    bias_full = lax.dynamic_update_slice(
        jnp.zeros((NB, part_heads * parts), f32), bias_own.T, (jnp.int32(0), t * part_heads + z * heads)
    )
    own_segments = lax.dynamic_slice_in_dim(segments, t * rows, rows)
    valid = (own_segments != 0).astype(f32)
    out_values = block_output.astype(f32)
    grad_values = input_grads.astype(f32)
    local_sums = jnp.stack(
        [
            jnp.sum(valid * jnp.sum(out_values * out_values, axis=1)),
            jnp.sum(valid * jnp.sum(grad_values * grad_values, axis=1)),
            jnp.sum(valid),
        ]
    )
    small = jnp.concatenate(
        [attn_gain_share, ff_gain_share, bias_full.reshape(-1), jnp.pad(local_sums, (0, BLOCK - 3))]
    ).reshape(-1, BLOCK)
    for axis in ("tensor", "dp", "ctx"):
        small = jnp.sum(gather_axis(small, axis), axis=0)
    back = tie(back, small, gate_out, up_out, down_out)
    at = output_sum.shape[2]
    output_out = jnp.sum(back[:, :, :at].astype(f32), axis=0).T
    query_out, key_out, value_out = own_rows(back[:, :, at:], (head_cols,) * 3)
    small = small.reshape(-1)
    gain_one_total, gain_two_total = small[:width], small[width : 2 * width]
    bias_total = small[2 * width : 2 * width + bias_full.size].reshape(bias_full.shape)
    sums_total = small[2 * width + bias_full.size :]
    rms_stats = jnp.sqrt(sums_total[:2] / (sums_total[2] * width))
    return (
        block_output,
        input_grads,
        gain_one_total,
        query_out,
        key_out,
        value_out,
        output_out,
        bias_total,
        gain_two_total,
        gate_out,
        up_out,
        down_out,
        rms_stats,
    )


def solution(mesh):
    return jax.shard_map(
        shards,
        mesh=mesh,
        in_specs=(
            P(("dp", "ctx", "tensor"), None),
            P(("dp", "ctx")),
            P(("dp", "ctx")),
            P(("dp", "ctx"), "tensor"),
            P(("dp", "ctx"), "tensor"),
            P(("dp", "ctx"), "tensor"),
            P("tensor", ("dp", "ctx")),
            P(None, "tensor"),
            P(("dp", "ctx")),
            P(("dp", "ctx"), "tensor"),
            P(("dp", "ctx"), "tensor"),
            P("tensor", ("dp", "ctx")),
            P(("dp", "ctx", "tensor"), None),
        ),
        out_specs=(
            P(("dp", "ctx", "tensor"), None),
            P(("dp", "ctx", "tensor"), None),
            P(),
            P(("dp", "ctx"), "tensor"),
            P(("dp", "ctx"), "tensor"),
            P(("dp", "ctx"), "tensor"),
            P("tensor", ("dp", "ctx")),
            P(),
            P(),
            P(("dp", "ctx"), "tensor"),
            P(("dp", "ctx"), "tensor"),
            P("tensor", ("dp", "ctx")),
            P(),
        ),
        check_vma=False,
    )
```

```python
import functools

import jax
import jax.numpy as jnp
from jax import lax
from jax.experimental import pallas as pl
from jax.experimental.pallas import tpu as pltpu
from jax.sharding import PartitionSpec as P

NB = 32
DH = 64
edge_list = (12, 16, 23, 32, 46, 64, 91)
exact_span = 8
eps = 1e-06
highest = lax.Precision.HIGHEST
bf16 = jnp.bfloat16
f32 = jnp.float32

TQ = 256
BLOCK = 128
CORES = 2
REACH = 128
SPAN = TQ + 2 * REACH
WIDE = 1024


def bucket_of(relative):
    distance = jnp.abs(relative)
    coarse = jnp.full_like(distance, exact_span)
    for edge in edge_list:
        coarse = coarse + (distance >= edge).astype(jnp.int32)
    nearby = jnp.where(distance < exact_span, distance, coarse)
    return nearby + jnp.where(relative > 0, NB // 2, 0)


def lane_buckets():
    lane = jnp.arange(WIDE, dtype=jnp.int32)
    ahead = jnp.where(lane < TQ, lane, lane - WIDE)
    onehot = bucket_of(-ahead - REACH)[:, None] == jnp.arange(NB, dtype=jnp.int32)[None, :]
    return onehot.astype(f32)


def dot_nt(a, b):
    return lax.dot_general(a, b, (((1,), (1,)), ((), ())), preferred_element_type=f32)


def dot_nn(a, b):
    return lax.dot_general(a, b, (((1,), (0,)), ((), ())), preferred_element_type=f32)


def tile_range(tile, seq_len):
    start = tile * TQ
    low, high = max(0, start - REACH), min(seq_len, start + TQ + REACH)
    return start, low, high, low - (start - REACH), high - (start - REACH)


def tile_scores(key, query, strip_ref, far, seg_col, seg_row, tile, seq_len):
    start, low, high, strip_low, strip_high = tile_range(tile, seq_len)
    scores = dot_nt(key, query)
    parts = []
    if low > 0:
        parts.append(scores[:low] + far[0])
    parts.append(scores[low:high] + strip_ref[strip_low:strip_high])
    if high < seq_len:
        parts.append(scores[high:] + far[1])
    scores = jnp.concatenate(parts, axis=0) if len(parts) > 1 else parts[0]
    return jnp.where(seg_col == seg_row[:, start : start + TQ], scores, -1e30)


def make_strip(strip_ref, vector):
    tall = jnp.broadcast_to(vector, (SPAN, WIDE))
    strip_ref[...] = pltpu.roll(tall, 0, 1, stride=1, stride_axis=0)[:, :TQ]


def fold_diagonals(acc_ref):
    rest = jnp.zeros((8, WIDE - TQ), f32)
    groups = jnp.zeros((8, WIDE), f32)
    for at in range(0, SPAN, 8):
        wide = jnp.concatenate([acc_ref[at : at + 8, :], rest], axis=1)
        groups = groups + pltpu.roll(wide, (WIDE - at) % WIDE, 1)
    diagonals = groups[0:1]
    for row in range(1, 8):
        diagonals = diagonals + pltpu.roll(groups[row : row + 1], WIDE - row, 1)
    return diagonals


def core_major(block, here, seq_len):
    core = lax.rem(block % CORES + CORES - here, CORES)
    return pl.ds(pl.multiple_of((core * (seq_len // BLOCK // CORES) + block // CORES) * BLOCK, BLOCK), BLOCK)


def piece_major(block, here):
    core = lax.rem(block % CORES + CORES - here, CORES)
    return pl.ds(pl.multiple_of((block // CORES * CORES + core) * BLOCK, BLOCK), BLOCK)


def attend_kernel(
    seq_len,
    here_ref,
    q_in,
    k_in,
    v_in,
    segc_ref,
    segr_ref,
    vec_ref,
    far_ref,
    mix_out,
    lse_ref,
    strip_ref,
    q_ref,
    k_ref,
    v_ref,
    mix_ref,
):
    seg_col = segc_ref[...]
    seg_row = segr_ref[...]
    pair = pl.program_id(0)
    here = here_ref[0]
    for block in range(seq_len // BLOCK):
        rows = slice(block * BLOCK, (block + 1) * BLOCK)
        source = core_major(block, here, seq_len)
        q_ref[rows], k_ref[rows], v_ref[rows] = q_in[source], k_in[source], v_in[source]
    value_t = v_ref[...].T
    for half in range(2):
        make_strip(strip_ref, vec_ref[0, half : half + 1, :])
        far = (far_ref[2 * pair + half, 0], far_ref[2 * pair + half, 1])
        lanes = slice(half * DH, (half + 1) * DH)
        key = k_ref[:, lanes]
        for tile in range(seq_len // TQ):
            rows = slice(tile * TQ, (tile + 1) * TQ)
            query = q_ref[rows, lanes]
            scores = tile_scores(key, query, strip_ref, far, seg_col, seg_row, tile, seq_len)
            top = jnp.max(scores, axis=0, keepdims=True)
            expo = jnp.exp(scores - top)
            total = jnp.sum(expo, axis=0, keepdims=True)
            mixed_t = dot_nn(value_t[lanes, :], expo.astype(bf16)) * (1.0 / total)
            mix_ref[rows, lanes] = mixed_t.T.astype(bf16)
            lse_ref[0, half : half + 1, rows] = top + jnp.log(total)
    for block in range(seq_len // BLOCK):
        mix_out[piece_major(block, here)] = mix_ref[block * BLOCK : (block + 1) * BLOCK]


def attend_back_kernel(
    seq_len,
    here_ref,
    q_in,
    k_in,
    v_in,
    do_in,
    segc_ref,
    segr_ref,
    vec_ref,
    far_ref,
    lse_ref,
    dqkv_out,
    diag_ref,
    farsum_ref,
    strip_ref,
    acc_ref,
    dk_acc,
    dv_acc,
    q_ref,
    k_ref,
    v_ref,
    do_ref,
    dq_ref,
    dk_ref,
    dv_ref,
):
    seg_col = segc_ref[...]
    seg_row = segr_ref[...]
    pair = pl.program_id(0)
    here = here_ref[0]
    for block in range(seq_len // BLOCK):
        rows = slice(block * BLOCK, (block + 1) * BLOCK)
        source = core_major(block, here, seq_len)
        q_ref[rows], k_ref[rows], v_ref[rows] = q_in[source], k_in[source], v_in[source]
        do_ref[rows] = do_in[piece_major(block, here)]
    key_t = k_ref[...].T
    for half in range(2):
        make_strip(strip_ref, vec_ref[0, half : half + 1, :])
        far = (far_ref[2 * pair + half, 0], far_ref[2 * pair + half, 1])
        lanes = slice(half * DH, (half + 1) * DH)
        key = k_ref[:, lanes]
        value = v_ref[:, lanes]
        acc_ref[...] = jnp.zeros_like(acc_ref)
        far_before = jnp.zeros((1, TQ), f32)
        far_after = jnp.zeros((1, TQ), f32)
        for tile in range(seq_len // TQ):
            start, low, high, strip_low, strip_high = tile_range(tile, seq_len)
            rows = slice(start, start + TQ)
            query = q_ref[rows, lanes]
            mixed_grad = do_ref[rows, lanes]
            scores = tile_scores(key, query, strip_ref, far, seg_col, seg_row, tile, seq_len)
            probs = jnp.exp(scores - lse_ref[0, half : half + 1, rows])
            prob_grad = dot_nt(value, mixed_grad)
            centre = jnp.sum(probs * prob_grad, axis=0, keepdims=True)
            score_grad = probs * (prob_grad - centre)
            rounded = score_grad.astype(bf16)
            value_g = dot_nn(probs.astype(bf16), mixed_grad)
            key_g = dot_nn(rounded, query)
            if tile == 0:
                dv_acc[...] = value_g
                dk_acc[...] = key_g
            else:
                dv_acc[...] += value_g
                dk_acc[...] += key_g
            dq_ref[rows, lanes] = dot_nn(key_t[lanes, :], rounded).T.astype(bf16)
            acc_ref[strip_low:strip_high, :] += score_grad[low:high]
            if low > 0:
                far_before = far_before + jnp.sum(score_grad[:low], axis=0, keepdims=True)
            if high < seq_len:
                far_after = far_after + jnp.sum(score_grad[high:], axis=0, keepdims=True)
        dk_ref[:, lanes] = dk_acc[...].astype(bf16)
        dv_ref[:, lanes] = dv_acc[...].astype(bf16)
        diag_ref[0, half : half + 1, :] = fold_diagonals(acc_ref)
        farsum_ref[0, half : half + 1, 0:TQ] = far_before
        farsum_ref[0, half : half + 1, TQ : 2 * TQ] = far_after
    for block in range(seq_len // BLOCK):
        rows = slice(block * BLOCK, (block + 1) * BLOCK)
        target = core_major(block, here, seq_len)
        for at, ref in enumerate((dq_ref, dk_ref, dv_ref)):
            start = (at * pl.num_programs(0) + pair) * (2 * DH)
            dqkv_out[target, pl.ds(pl.multiple_of(start, 2 * DH), 2 * DH)] = ref[rows]


def kernel_params():
    return pltpu.CompilerParams(vmem_limit_bytes=56 * 1024 * 1024)


def attention_specs(seq_len, pairs):
    wide = lambda at: pl.BlockSpec((seq_len, 2 * DH), lambda p, at=at: (0, at * pairs + p))
    seg_c = pl.BlockSpec((seq_len, 1), lambda p: (0, 0))
    seg_r = pl.BlockSpec((1, seq_len), lambda p: (0, 0))
    vec = pl.BlockSpec((1, 2, WIDE), lambda p: (p, 0, 0))
    far = pl.BlockSpec(memory_space=pltpu.SMEM)
    lse = pl.BlockSpec((1, 2, seq_len), lambda p: (p, 0, 0))
    return wide, seg_c, seg_r, vec, far, lse


def attend(here, qkv, segs, vectors, far):
    seq_len = qkv.shape[0]
    pairs = vectors.shape[0]
    wide, seg_c, seg_r, vec, far_spec, lse = attention_specs(seq_len, pairs)
    work = pairs * 2 * seq_len * seq_len
    return pl.pallas_call(
        functools.partial(attend_kernel, seq_len),
        grid=(pairs,),
        in_specs=[far_spec, wide(0), wide(1), wide(2), seg_c, seg_r, vec, far_spec],
        out_specs=[wide(0), lse],
        out_shape=[
            jax.ShapeDtypeStruct((seq_len, pairs * 2 * DH), bf16),
            jax.ShapeDtypeStruct((pairs, 2, seq_len), f32),
        ],
        scratch_shapes=[pltpu.VMEM((SPAN, TQ), f32)] + [pltpu.VMEM((seq_len, 2 * DH), bf16)] * 4,
        compiler_params=kernel_params(),
        cost_estimate=pl.CostEstimate(
            flops=16 * DH * work, bytes_accessed=8 * seq_len * pairs * DH, transcendentals=work
        ),
        name="attend",
    )(here, qkv, qkv, qkv, segs[:, None], segs[None, :], vectors, far)


def attend_back(here, qkv, mixed_grad, segs, vectors, far, lse_rows):
    seq_len = qkv.shape[0]
    pairs = vectors.shape[0]
    wide, seg_c, seg_r, vec, far_spec, lse = attention_specs(seq_len, pairs)
    work = pairs * 2 * seq_len * seq_len
    dqkv_shape = (seq_len, pairs * 6 * DH)
    return pl.pallas_call(
        functools.partial(attend_back_kernel, seq_len),
        grid=(pairs,),
        in_specs=[far_spec, wide(0), wide(1), wide(2), wide(0), seg_c, seg_r, vec, far_spec, lse],
        out_specs=[
            pl.BlockSpec(dqkv_shape, lambda p: (0, 0)),
            vec,
            pl.BlockSpec((1, 2, 2 * TQ), lambda p: (p, 0, 0)),
        ],
        out_shape=[
            jax.ShapeDtypeStruct(dqkv_shape, bf16),
            jax.ShapeDtypeStruct((pairs, 2, WIDE), f32),
            jax.ShapeDtypeStruct((pairs, 2, 2 * TQ), f32),
        ],
        scratch_shapes=[
            pltpu.VMEM((SPAN, TQ), f32),
            pltpu.VMEM((SPAN, TQ), f32),
            pltpu.VMEM((seq_len, DH), f32),
            pltpu.VMEM((seq_len, DH), f32),
        ]
        + [pltpu.VMEM((seq_len, 2 * DH), bf16)] * 7,
        compiler_params=kernel_params(),
        cost_estimate=pl.CostEstimate(
            flops=40 * DH * work, bytes_accessed=16 * seq_len * pairs * DH, transcendentals=work
        ),
        name="attend_back",
    )(here, qkv, qkv, qkv, mixed_grad, segs[:, None], segs[None, :], vectors, far, lse_rows)


def shift(value, axis, by):
    size = lax.axis_size(axis)
    return lax.ppermute(value, axis, [(i, (i + by) % size) for i in range(size)])


def block_at(stack, at):
    return lax.dynamic_index_in_dim(stack, at, 0, keepdims=False)


def place(stack, block, at):
    return lax.dynamic_update_slice(stack, block[None], (at,) + (jnp.int32(0),) * block.ndim)


def arrivals(block, axis):
    return [shift(block, axis, k) for k in range(1, lax.axis_size(axis))]


def assemble(block, arrived, axis):
    size, me = lax.axis_size(axis), lax.axis_index(axis)
    stack = place(jnp.zeros((size,) + block.shape, block.dtype), block, me)
    for k in range(1, size):
        stack = place(stack, arrived[k - 1], (me - k) % size)
    return stack


def gather_axis(block, axis):
    return assemble(block, arrivals(block, axis), axis)


def flip(value, mask):
    size = lax.axis_size("dp")
    return lax.ppermute(value, "dp", [(i, i ^ mask) for i in range(size)])


def gather_rows(block):
    if lax.axis_size("dp") != 4:
        return flat(gather_axis(block, "dp"))
    me, half = lax.axis_index("dp"), block.shape[0] // 2
    near, other = flip(block, 1), flip(block, 2)
    first, second = flip(near[:half], 2), flip(other[half:], 1)
    stack = place(jnp.zeros((4,) + block.shape, block.dtype), block, me)
    stack = place(place(stack, near, me ^ 1), other, me ^ 2)
    zero = jnp.int32(0)
    stack = lax.dynamic_update_slice(stack, first[None], (me ^ 3, zero, zero))
    stack = lax.dynamic_update_slice(stack, second[None], (me ^ 3, jnp.int32(half), zero))
    return flat(stack)


def exchange_axis(block_of, axis):
    size, me = lax.axis_size(axis), lax.axis_index(axis)
    own = block_of(me)
    stack = place(jnp.zeros((size,) + own.shape, own.dtype), own, me)
    for k in range(1, size):
        stack = place(stack, shift(block_of((me + k) % size), axis, k), (me - k) % size)
    return stack


def scatter_sum_axis(block_of, axis):
    size, me = lax.axis_size(axis), lax.axis_index(axis)
    arrived = [shift(block_of((me + k) % size).astype(bf16), axis, k) for k in range(1, size)]
    total = block_of(me).astype(f32)
    for block in arrived:
        total = total + block.astype(f32)
    return total


def tie(value, *others):
    return lax.optimization_barrier((value,) + others)[0]


def swap(block):
    return shift(block, "tensor", 1)


def exchange(stack, axis):
    return lax.all_to_all(stack, axis, 0, 0)


def gather_bcast(rows, axis):
    return exchange(jnp.broadcast_to(rows[None], (lax.axis_size(axis),) + rows.shape), axis)


def gather_tokens(rows, axis):
    return both_cores(gather_bcast(rows, axis))


def both_cores(stack):
    return jnp.concatenate([stack, swap(stack)], axis=0).reshape(-1, stack.shape[-1])


def sum_of_cores(partial, axis):
    stack = partial.reshape(CORES, lax.axis_size(axis), -1, partial.shape[-1])
    return (stack[0].astype(f32) + swap(stack[1].astype(bf16)).astype(f32)).astype(bf16)


def sum_of_axis(stack, axis):
    return jnp.sum(exchange(stack, axis).astype(f32), axis=0)


def columns_in(matrix, order):
    wide = matrix.shape[1] // len(order)
    return jnp.concatenate([matrix[:, j * wide : (j + 1) * wide] for j in order], axis=1)


def by_piece(matrix):
    dps, pieces = lax.axis_size("dp"), lax.axis_size("ctx")
    return columns_in(matrix, [j * pieces + i for i in range(pieces) for j in range(dps)])


def by_dp(matrix):
    dps, pieces = lax.axis_size("dp"), lax.axis_size("ctx")
    return columns_in(matrix, [i * dps + j for j in range(dps) for i in range(pieces)])


def piece_columns(weights):
    pieces = lax.axis_size("ctx")
    split = [jnp.transpose(w.reshape(w.shape[0], pieces, -1), (1, 0, 2)) for w in weights]
    return jnp.concatenate(split, axis=2)


def own_rows(stack, widths):
    outs, at = [], 0
    for width in widths:
        part = stack[:, :, at : at + width].astype(f32)
        outs.append(jnp.transpose(part, (1, 0, 2)).reshape(part.shape[1], -1))
        at += width
    return outs


def send_weight(left, right):
    size, me = lax.axis_size("dp"), lax.axis_index("dp")
    wide = left.shape[1] // size

    def block_of(j):
        return mm_tn(lax.dynamic_slice_in_dim(left, j * wide, wide, 1), right)

    arrived = [shift(block_of((me + k) % size).astype(bf16), "dp", k) for k in range(1, size)]
    return block_of(me), arrived


def sum_weight(own, arrived):
    for block in arrived:
        own = own + block.astype(f32)
    return own.astype(bf16).reshape(lax.axis_size("ctx"), -1, own.shape[1])


def reduce_weight(left, right):
    if lax.axis_size("dp") != 4:
        own, arrived = send_weight(left, right)
        return sum_weight(own, arrived), arrived
    me, wide, half = lax.axis_index("dp"), left.shape[1] // 4, right.shape[1] // 2

    def block_of(j):
        return mm_tn(lax.dynamic_slice_in_dim(left, j * wide, wide, 1), right)

    far = block_of(me ^ 3).astype(bf16)
    near = block_of(me ^ 1).astype(bf16)
    other = block_of(me ^ 2).astype(bf16)
    from_near = flip(jnp.stack([near[:, :half], far[:, :half]]), 1)
    from_other = flip(jnp.stack([other[:, half:], far[:, half:]]), 2)
    own = block_of(me)
    low = flip((other[:, :half].astype(f32) + from_near[1].astype(f32)).astype(bf16), 2)
    high = flip((near[:, half:].astype(f32) + from_other[1].astype(f32)).astype(bf16), 1)
    low = own[:, :half] + from_near[0].astype(f32) + low.astype(f32)
    high = own[:, half:] + from_other[0].astype(f32) + high.astype(f32)
    return sum_weight(jnp.concatenate([low, high], axis=1), []), [from_near, from_other]


def flat(stack):
    return stack.reshape(-1, stack.shape[-1])


def root_mean_square_backward(grad, normalized, scale, gain):
    scaled = grad * gain
    return scale * (scaled - normalized * jnp.mean(scaled * normalized, axis=-1, keepdims=True))


def mm(a, b):
    return jnp.dot(a, b, preferred_element_type=f32)


def mm_nt(a, b):
    return dot_nt(a, b)


def mm_tn(a, b):
    return lax.dot_general(a, b, (((0,), (0,)), ((), ())), preferred_element_type=f32)


def inverse_scale(values):
    return lax.rsqrt(jnp.mean(values * values, axis=1, keepdims=True) + eps)


def shards(
    layer_input,
    segments,
    attn_gain,
    query_weight,
    key_weight,
    value_weight,
    output_weight,
    bias_table,
    ff_gain,
    gate_weight,
    up_weight,
    down_weight,
    cotangent,
):
    parts, pieces, dps = lax.axis_size("tensor"), lax.axis_size("ctx"), lax.axis_size("dp")
    t, z, s = lax.axis_index("tensor"), lax.axis_index("ctx"), lax.axis_index("dp")
    rows, width = layer_input.shape
    seq_len = rows * parts * pieces
    part_heads = bias_table.shape[1]
    heads = part_heads // pieces
    head_cols = heads * DH


    here = jnp.reshape(t, (1,)).astype(jnp.int32)

    x_core = lax.all_gather(layer_input, "ctx", axis=0)
    small_in = jnp.concatenate([attn_gain, ff_gain, segments.astype(bf16)]).reshape(1, -1)
    small_pieces = gather_axis(small_in, "ctx").reshape(pieces, -1)
    gain_cols = attn_gain.shape[0]
    segs = small_pieces[:, 2 * gain_cols :].astype(jnp.int32).reshape(seq_len)
    attn_blocks = piece_columns([query_weight, key_weight, value_weight])
    out_block = jnp.broadcast_to(output_weight.T[None], (pieces, output_weight.shape[1], part_heads * DH))
    attn_blocks = jnp.concatenate([attn_blocks, out_block], axis=2)
    attn_pieces = flat(exchange(tie(attn_blocks, small_pieces), "ctx"))

    units = down_weight.shape[0] // dps
    ff_weights = (gate_weight, up_weight, down_weight.T)
    ff_weights = lax.optimization_barrier(ff_weights + (small_pieces,))[:3]

    def ff_block(j):
        columns = [lax.dynamic_slice_in_dim(w, j * units, units, 1) for w in ff_weights]
        return jnp.concatenate(columns, axis=1)

    ff_arrived = [shift(ff_block((s + k) % dps), "dp", k) for k in range(1, dps)]
    gains = gather_axis(tie(small_pieces, *ff_arrived)[:, : 2 * gain_cols], "dp")
    gains = gains.reshape(dps, pieces, 2, gain_cols)
    gains = jnp.transpose(gains, (2, 0, 1, 3)).reshape(2, width).astype(f32)
    gain_one, gain_two = gains[0:1], gains[1:2]
    dy_own = by_piece(cotangent)
    dy_arrived = arrivals(tie(dy_own, *ff_arrived), "dp")
    attn_pieces = tie(attn_pieces, gains, *ff_arrived, *dy_arrived)
    ff_rows = assemble(ff_block(s), ff_arrived, "dp")
    w_ff = lax.all_gather(flat(ff_rows), "ctx", axis=0, tiled=True)
    w_gu, w_down = w_ff[:, : 2 * units], w_ff[:, 2 * units :]

    w_qkv = gather_rows(attn_pieces[:, : 3 * head_cols])
    x_seq = both_cores(x_core)

    own_table = lax.dynamic_slice_in_dim(bias_table, z * heads, heads, 1)
    lanes_onehot = lane_buckets()
    vectors = jnp.dot(lanes_onehot, own_table, precision=highest).T.reshape(heads // 2, 2, WIDE)
    far = jnp.stack([own_table[NB // 2 - 1], own_table[NB - 1]], axis=1)

    x_wide = tie(x_seq, w_qkv).astype(f32)
    normed_seq = (x_wide * inverse_scale(x_wide) * gain_one).astype(bf16)
    qkv = mm(normed_seq, w_qkv).astype(bf16)
    w_out = gather_rows(tie(attn_pieces, qkv)[:, 3 * head_cols :])
    mixed_heads, lse_rows = attend(here, qkv, segs, vectors, far)
    mixed = exchange(mixed_heads.reshape(pieces, parts * rows, head_cols), "ctx")
    dy_all = both_cores(assemble(tie(dy_own, qkv), dy_arrived, "dp"))
    mixed = jnp.transpose(mixed, (1, 0, 2)).reshape(rows * parts, -1)
    attn_part = mm_nt(mixed, w_out)
    attn_own = attn_part[:rows] + swap(attn_part[rows:].astype(bf16)).astype(f32)

    x_own = layer_input.astype(f32)
    scale_one = inverse_scale(x_own)
    unit_one = x_own * scale_one
    hidden = x_own + attn_own
    scale_two = inverse_scale(hidden)
    unit_two = hidden * scale_two
    normed_two = (unit_two * gain_two).astype(bf16)

    normed_two_all = gather_tokens(tie(by_piece(normed_two), dy_all), "dp")
    gate_up = mm(normed_two_all, w_gu)
    inner_grad = mm(dy_all, w_down)
    gate, upper = gate_up[:, :units], gate_up[:, units:]
    inner, gelu_pull = jax.vjp(lambda g, u: jax.nn.gelu(g, approximate=True) * u, gate, upper)
    inner = inner.astype(bf16)
    gate_grad, upper_grad = gelu_pull(inner_grad)
    gate_up_grad = jnp.concatenate([gate_grad.astype(bf16), upper_grad.astype(bf16)], axis=1)
    normed_two_part = mm_nt(gate_up_grad, w_gu).astype(bf16)
    normed_two_core = sum_of_cores(normed_two_part, "dp")
    normed_two_sum = sum_of_axis(normed_two_core, "dp")
    gate_up_late, inner_late = lax.optimization_barrier(
        (gate_up_grad, inner, normed_two_core)
    )[:2]
    down_wgrad = mm_tn(dy_all, inner).astype(bf16)
    down_sum = lax.psum_scatter(down_wgrad, "ctx", scatter_dimension=0, tiled=True)
    gu_wgrad = mm_tn(normed_two_all, gate_up_late).astype(bf16)
    gu_sum = lax.psum_scatter(gu_wgrad, "ctx", scatter_dimension=0, tiled=True)
    normed_two_sum = tie(normed_two_sum, gu_wgrad)
    normed_two_sum = by_dp(normed_two_sum)
    normed_two_grad = normed_two_sum

    ff_gain_share = jnp.sum(normed_two_grad * unit_two, axis=0)
    hidden_grad = cotangent.astype(f32) + root_mean_square_backward(
        normed_two_grad, unit_two, scale_two, gain_two
    )
    attn_step = hidden_grad.astype(bf16)
    attn_step = jnp.concatenate([attn_step, swap(attn_step)], axis=0)
    mixed_grad = mm(attn_step, w_out).astype(bf16).reshape(rows * parts, pieces, head_cols)
    mixed_grad = flat(exchange(jnp.transpose(mixed_grad, (1, 0, 2)), "ctx"))
    output_sum, output_arrived = reduce_weight(attn_step, mixed)
    ff_part = mm_nt(tie(inner_late, attn_step), w_down).astype(bf16)
    ff_core = sum_of_cores(ff_part, "dp")
    ff_stack = exchange(tie(ff_core, mixed_grad), "dp")

    mixed_grad = tie(mixed_grad, down_sum, output_arrived[1])
    dqkv, diagonals, far_sums = attend_back(
        here, qkv, mixed_grad, segs, vectors, far, lse_rows
    )
    dqkv = tie(dqkv, ff_stack, output_sum)
    normed_one_part = mm_nt(dqkv, w_qkv).astype(bf16)
    normed_one_core = sum_of_cores(normed_one_part, "ctx")
    normed_one_sum = sum_of_axis(normed_one_core, "ctx")
    ff_own = by_dp(jnp.sum(tie(ff_stack, normed_one_core).astype(f32), axis=0))
    block_output = (hidden + ff_own).astype(bf16)
    qkv_sum, _ = reduce_weight(normed_seq, tie(dqkv, normed_one_core))
    ff_blocks = jnp.concatenate([gu_sum, down_sum], axis=1)
    ff_blocks = tie(ff_blocks, qkv_sum).reshape(dps, -1, 3 * units)
    ff_back = exchange_axis(lambda j: block_at(ff_blocks, j), "dp")
    gate_out, up_out, down_out = own_rows(ff_back, (units,) * 3)
    down_out = down_out.T
    normed_one_grad = tie(normed_one_sum, block_output, ff_back)
    sums = jnp.concatenate([output_sum, qkv_sum], axis=2)
    back = exchange(tie(sums, normed_one_sum), "ctx")
    attn_gain_share = jnp.sum(normed_one_grad * unit_one, axis=0)
    input_grads = (
        hidden_grad + root_mean_square_backward(normed_one_grad, unit_one, scale_one, gain_one)
    ).astype(bf16)

    far_total = jnp.sum(far_sums.reshape(heads, 2, TQ), axis=2)
    bias_own = jnp.dot(diagonals.reshape(heads, WIDE), lanes_onehot, precision=highest)
    bucket = jnp.arange(NB, dtype=jnp.int32)[None, :]
    bias_own = bias_own + jnp.where(bucket == NB // 2 - 1, far_total[:, 0:1], 0.0)
    bias_own = bias_own + jnp.where(bucket == NB - 1, far_total[:, 1:2], 0.0)
    bias_full = lax.dynamic_update_slice(
        jnp.zeros((NB, part_heads * parts), f32), bias_own.T, (jnp.int32(0), t * part_heads + z * heads)
    )
    own_segments = lax.dynamic_slice_in_dim(segments, t * rows, rows)
    valid = (own_segments != 0).astype(f32)
    out_values = block_output.astype(f32)
    grad_values = input_grads.astype(f32)
    local_sums = jnp.stack(
        [
            jnp.sum(valid * jnp.sum(out_values * out_values, axis=1)),
            jnp.sum(valid * jnp.sum(grad_values * grad_values, axis=1)),
            jnp.sum(valid),
        ]
    )
    small = jnp.concatenate(
        [attn_gain_share, ff_gain_share, bias_full.reshape(-1), jnp.pad(local_sums, (0, BLOCK - 3))]
    ).reshape(-1, BLOCK)
    for axis in ("tensor", "dp", "ctx"):
        small = jnp.sum(gather_axis(small, axis), axis=0)
    back = tie(back, small, gate_out, up_out, down_out)
    at = output_sum.shape[2]
    output_out = jnp.sum(back[:, :, :at].astype(f32), axis=0).T
    query_out, key_out, value_out = own_rows(back[:, :, at:], (head_cols,) * 3)
    small = small.reshape(-1)
    gain_one_total, gain_two_total = small[:width], small[width : 2 * width]
    bias_total = small[2 * width : 2 * width + bias_full.size].reshape(bias_full.shape)
    sums_total = small[2 * width + bias_full.size :]
    rms_stats = jnp.sqrt(sums_total[:2] / (sums_total[2] * width))
    return (
        block_output,
        input_grads,
        gain_one_total,
        query_out,
        key_out,
        value_out,
        output_out,
        bias_total,
        gain_two_total,
        gate_out,
        up_out,
        down_out,
        rms_stats,
    )


def solution(mesh):
    return jax.shard_map(
        shards,
        mesh=mesh,
        in_specs=(
            P(("dp", "ctx", "tensor"), None),
            P(("dp", "ctx")),
            P(("dp", "ctx")),
            P(("dp", "ctx"), "tensor"),
            P(("dp", "ctx"), "tensor"),
            P(("dp", "ctx"), "tensor"),
            P("tensor", ("dp", "ctx")),
            P(None, "tensor"),
            P(("dp", "ctx")),
            P(("dp", "ctx"), "tensor"),
            P(("dp", "ctx"), "tensor"),
            P("tensor", ("dp", "ctx")),
            P(("dp", "ctx", "tensor"), None),
        ),
        out_specs=(
            P(("dp", "ctx", "tensor"), None),
            P(("dp", "ctx", "tensor"), None),
            P(),
            P(("dp", "ctx"), "tensor"),
            P(("dp", "ctx"), "tensor"),
            P(("dp", "ctx"), "tensor"),
            P("tensor", ("dp", "ctx")),
            P(),
            P(),
            P(("dp", "ctx"), "tensor"),
            P(("dp", "ctx"), "tensor"),
            P("tensor", ("dp", "ctx")),
            P(),
        ),
        check_vma=False,
    )
```
